128 devices in a mesh: row: 8 (over z, core), col: 16 (over x, y).
Axes of the slice: x: 4, y: 4, z: 4, core: 2. Of those that a mesh axis runs over, the one named last changes fastest.
Arguments:
- basis_values: bfloat16 [128, 1536, 1024], P(('row', 'col')), may hold values from -6 to 6
- quad_weights: float32 [128, 1536], P(('row', 'col')), may hold values from 0.0001953125 to 0.001953125
- point_counts: int32 [128], P(('row', 'col')), may hold values from 192 to 1536, as said below
- basis_tiles: int32 [128, 8], replicated, may hold values from 0 to 47, as said below
- density: bfloat16 [6144, 6144], P('row', 'col'), may hold values from -0.005859375 to 0.005859375
- core_matrix: float32 [6144, 6144], P('row', 'col'), as said below
- map_shift: float32 [1], replicated, may hold values from 0.2 to 0.6
- map_scale: float32 [1], replicated, may hold values from -0.05 to -0.03
- branch_flags: int32 [1], replicated, may hold values from 0 to 1
Outputs:
- point_density: float32 [128, 1536], P(('row', 'col'))
- xc_potential: float32 [6144, 6144], P('row', 'col')
- purified: float32 [6144, 6144], P('row', 'col')
The draws below stay inside these ranges and needn't reach their ends.
Inputs may be any that keep to these rules, and one draw needn't show every extreme that they name: `basis_tiles`: entry j of every row lies in j * 6 to (j + 1) * 6 - 1. The first point_counts[q] points of batch q are live; some batch has all 1536 live. `core_matrix`: a symmetric matrix.
All inputs are finite; a program needn't handle non-finite values.
Results may differ from the reference program's by a relative error of at most 0.0067.
Values may be sent and summed in bfloat16 or wider, within the bound.
A program may use at most 64 MiB of HBM per device.

```python
import math
import jax
import jax.numpy as jnp
from jax import lax

M = 6144
TILE = 128
NB = 1024
G = 1536
BLK = 8
BS = 6
BATCHES = 128


def draw_basis_tiles(key, part):
    key = jax.random.fold_in(key, 11)
    offsets = jax.random.randint(key, (BATCHES, BLK), 0, BS)
    return (jnp.arange(BLK, dtype=jnp.int32)[None, :] * BS + offsets).astype(jnp.int32)


def draw_point_counts(key, part):
    key = jax.random.fold_in(key, 23)
    counts = jax.random.randint(key, (BATCHES,), G // 8, G + 1)
    where_full = jax.random.randint(jax.random.fold_in(key, 5), (), 0, BATCHES)
    return counts.at[where_full].set(G).astype(jnp.int32)


def draw_core_matrix(key, part):
    key = jax.random.fold_in(key, 37)
    raw = jax.random.normal(key, (M, M), jnp.float32)
    return ((raw + raw.T) * 0.35).astype(jnp.float32)


def levels(stream_key, dims, split, smallest, high):
    level, own = 1.0, jax.random.fold_in(stream_key, 6)
    for position, blocks in split:
        heights = jnp.exp(jax.random.uniform(jax.random.fold_in(own, position), (blocks,), jnp.float32, smallest / len(split), high / len(split)))
        level = level * jnp.repeat(heights, dims[position] // blocks).reshape([-1 if axis == position else 1 for axis in range(len(dims))])
    return level


def normal_values(key, dims, scale, reach, pieces=(), kind=jnp.bfloat16):
    result = jax.random.normal(key, dims, jnp.float32) * scale
    if len(pieces) > 0:
        result = levels(key, dims, pieces, -0.22, 0.18) * result
    return jnp.clip(result, min=-reach, max=reach).astype(kind)


def setup_inputs(seed: int = 0) -> dict:
    key_of = jax.random.split(jax.random.key(seed), 10)
    basis_values = normal_values(key_of[0], (BATCHES, G, NB), 1.0, 6.0, ((0, 128),))
    quad_weights = jnp.clip(jnp.exp(math.log(0.001953125) - 2.3025851 * jax.random.uniform(key_of[1], (BATCHES, G), jnp.float32) ** levels(key_of[1], (BATCHES, G), ((0, 128),), -0.2, 0.2)), 0.0001953125, 0.001953125)
    point_counts = draw_point_counts(jax.random.fold_in(key_of[9], 71), 0)
    basis_tiles = draw_basis_tiles(jax.random.fold_in(key_of[9], 71), 0)
    density = normal_values(key_of[4], (M, M), (NB * NB) ** -0.5, 0.005859375, ((0, 8), (1, 16)))
    core_matrix = draw_core_matrix(jax.random.fold_in(key_of[9], 71), 0)
    map_shift = jnp.clip(jax.random.uniform(key_of[6], (1,), jnp.float32, 0.2, 0.6), 0.2, 0.6)
    map_scale = jnp.clip(jax.random.uniform(key_of[7], (1,), jnp.float32, -0.05, -0.03), -0.05, -0.03)
    branch_flags = jax.random.randint(key_of[8], (1,), 0, 2).astype(jnp.int32)
    return {"basis_values": basis_values, "quad_weights": quad_weights, "point_counts": point_counts, "basis_tiles": basis_tiles, "density": density, "core_matrix": core_matrix, "map_shift": map_shift, "map_scale": map_scale, "branch_flags": branch_flags}


SLATER = (3.0 / 3.141592653589793) ** (1.0 / 3.0)


def potential_factor(values):
    return -SLATER * (values * values + 1.0) ** (1.0 / 6.0)


def reference(basis_values, quad_weights, point_counts, basis_tiles, density, core_matrix, map_shift, map_scale, branch_flags):
    offsets = jnp.arange(TILE, dtype=jnp.int32)
    point_ids = jnp.arange(G, dtype=jnp.int32)

    def one_batch(potential, inputs):
        values, weights, count, tiles = inputs
        index = (tiles[:, None].astype(jnp.int32) * TILE + offsets[None, :]).reshape(-1).astype(jnp.int32)
        submatrix = density[index[:, None], index[None, :]]
        mixed = jnp.dot(values, submatrix, preferred_element_type=jnp.float32)
        local_density = jnp.sum(mixed * values.astype(jnp.float32), axis=1)
        live = point_ids < count
        local_density = jnp.where(live, local_density, jnp.float32(0.0))
        factor = jnp.where(live, weights * potential_factor(local_density), jnp.float32(0.0))
        weighted = (factor[:, None] * values).astype(jnp.bfloat16)
        block = jnp.dot(values.T, weighted, preferred_element_type=jnp.float32)
        potential = potential.at[index[:, None], index[None, :]].add(block)
        return potential, local_density

    potential, densities = lax.scan(one_batch, jnp.zeros((M, M), jnp.float32), (basis_values, quad_weights, point_counts, basis_tiles))
    identity = jnp.eye(M, dtype=jnp.float32)
    start = map_shift[0] * identity + map_scale[0] * (core_matrix + potential)
    rounded = start.astype(jnp.bfloat16)
    square = jnp.dot(rounded, rounded, preferred_element_type=jnp.float32)
    purified = jnp.where(branch_flags[0] == 0, square, 2.0 * start - square)
    return densities, potential, purified
```

```python
import jax
import jax.numpy as jnp
from jax import lax
from jax.experimental import pallas as pl
from jax.experimental.pallas import tpu as pltpu
from jax.sharding import PartitionSpec as P

MESH = pl.DeviceIdType.MESH
TILE = 128
RING = 4


def turn(value, step):
    return lax.rem(value + (step % RING), RING)


def square_kernel(
    own_ref, start_ref, mix_ref, out_ref, rows_ref, cols_ref, row_send, row_recv, col_send, col_recv, core_send, core_recv, own_sem
):
    row, col = lax.axis_index("row"), lax.axis_index("col")
    z, core = row // 2, lax.rem(row, 2)
    x, y = col // RING, lax.rem(col, RING)
    tall, wide = own_ref.shape
    half = tall // 2
    quarter = half // 2

    def device(axis, step):
        if axis == "x":
            return (row, turn(x, step) * RING + y)
        if axis == "y":
            return (row, x * RING + turn(y, step))
        if axis == "z":
            return (turn(z, step) * 2 + core, col)
        return (z * 2 + 1 - core, col)

    def hop(place):
        position, part = place
        if position == 3:
            return 1, 0
        if position == 1:
            return -1, 0
        return (1, 3) if part == 0 else (-1, 1)

    def row_block(side, dx, dy):
        if dx == 0 and dy == 0:
            return own_ref.at[pl.ds(side * half, half)]
        return rows_ref.at[side, dx, dy]

    def row_copy(side, dx, dy, part=0):
        first, second = (dx, dy) if side == 0 else (dy, dx)
        axes = ("x", "y") if side == 0 else ("y", "x")
        place = second if second else first
        axis = axes[1] if second else axes[0]
        step, source = hop((place, part))
        origin = (first, source) if second else (source, 0)
        sx, sy = origin if side == 0 else origin[::-1]
        src, dst = row_block(side, sx, sy), rows_ref.at[side, dx, dy]
        if place == 2:
            cut = pl.ds(part * quarter, quarter)
            src, dst = src.at[cut], dst.at[cut]
        return pltpu.make_async_remote_copy(
            src_ref=src,
            dst_ref=dst,
            send_sem=row_send.at[side, dx, dy, part],
            recv_sem=row_recv.at[side, dx, dy, part],
            device_id=device(axis, step),
            device_id_type=MESH,
        )

    def col_copy(dz, part=0):
        step, source = hop((dz, part))
        slot = turn(z, source)
        src = own_ref if source == 0 else cols_ref.at[slot, core]
        dst = cols_ref.at[slot, core]
        if dz == 2:
            cut = pl.ds(part * half, half)
            src, dst = src.at[cut], dst.at[cut]
        return pltpu.make_async_remote_copy(
            src_ref=src,
            dst_ref=dst,
            send_sem=col_send.at[dz, part],
            recv_sem=col_recv.at[dz, part],
            device_id=device("z", step),
            device_id_type=MESH,
        )

    def core_copy(dz):
        slot = turn(z, dz)
        return pltpu.make_async_remote_copy(
            src_ref=own_ref if dz == 0 else cols_ref.at[slot, core],
            dst_ref=cols_ref.at[slot, core],
            send_sem=core_send.at[dz],
            recv_sem=core_recv.at[dz],
            device_id=device("core", 1),
            device_id_type=MESH,
        )

    def row_pair(side, first, second):
        return (first, second) if side == 0 else (second, first)

    barrier = pltpu.get_barrier_semaphore()
    partners = [device(a, s) for a in ("x", "y", "z") for s in (1, -1)] + [device("core", 1)]
    for partner in partners:
        pl.semaphore_signal(barrier, inc=1, device_id=partner, device_id_type=MESH)
    pl.semaphore_wait(barrier, len(partners))

    started = []

    def go(copy):
        copy.start()
        started.append(copy)

    for place in (3, 1):
        for side in (0, 1):
            go(row_copy(side, *row_pair(side, place, 0)))
    for place in (3, 1):
        go(col_copy(place))
    go(core_copy(0))
    for place in (3, 1):
        for side in (0, 1):
            go(row_copy(side, *row_pair(side, 0, place)))
    mine = pltpu.make_async_copy(own_ref, cols_ref.at[z, core], own_sem)
    mine.start()

    for place, part in ((3, 0), (1, 1)):
        for side in (0, 1):
            row_copy(side, *row_pair(side, place, 0)).wait_recv()
            go(row_copy(side, *row_pair(side, 2, 0), part))
        for side in (0, 1):
            for second in (3, 1):
                go(row_copy(side, *row_pair(side, place, second)))
        col_copy(place).wait_recv()
        go(col_copy(2, part))
        go(core_copy(place))
    for side in (0, 1):
        for part in (0, 1):
            row_copy(side, *row_pair(side, 2, 0), part).wait_recv()
        for second in (3, 1):
            go(row_copy(side, *row_pair(side, 2, second)))
    for part in (0, 1):
        col_copy(2, part).wait_recv()
    go(core_copy(2))

    def second_ring(first):
        for place, part in ((3, 0), (1, 1)):
            for side in (0, 1):
                row_copy(side, *row_pair(side, first, place)).wait_recv()
                go(row_copy(side, *row_pair(side, first, 2), part))

    def multiply(side, dx, dy):
        index = turn(x, dx) * RING + turn(y, dy)
        owner, cut = index // 2, lax.rem(index, 2)
        factor = cols_ref[owner // 2, lax.rem(owner, 2), pl.ds(pl.multiple_of(cut * wide, wide), wide), :]
        product = jnp.dot(row_block(side, dx, dy)[...], factor, preferred_element_type=jnp.float32)
        spot = pl.ds(side * half, half)
        if dx == 0 and dy == 0:
            out_ref[spot, :] = product
        else:
            out_ref[spot, :] += product

    second_ring(0)
    mine.wait()
    for dz in range(RING):
        core_copy(dz).wait_recv()
    for side in (0, 1):
        for first in range(RING):
            multiply(side, *row_pair(side, first, 0))
        for place in (3, 1):
            multiply(side, *row_pair(side, 0, place))
    for first in (3, 1, 2):
        second_ring(first)
        for side in (0, 1):
            for place in (3, 1):
                multiply(side, *row_pair(side, first, place))
    for first in (0, 3, 1, 2):
        for side in (0, 1):
            for part in (0, 1):
                row_copy(side, *row_pair(side, first, 2), part).wait_recv()
            multiply(side, *row_pair(side, first, 2))
    out_ref[...] = mix_ref[0] * out_ref[...] + mix_ref[1] * start_ref[...]
    for copy in started:
        copy.wait_send()


def squared(rounded, start, mix):
    tall, wide = rounded.shape
    vmem = pl.BlockSpec(memory_space=pltpu.VMEM)
    dma = pltpu.SemaphoreType.DMA
    return pl.pallas_call(
        square_kernel,
        name="square_kernel",
        out_shape=jax.ShapeDtypeStruct((tall, wide), jnp.float32),
        in_specs=[vmem, vmem, pl.BlockSpec(memory_space=pltpu.SMEM)],
        out_specs=vmem,
        scratch_shapes=[
            pltpu.VMEM((2, RING, RING, tall // 2, wide), jnp.bfloat16),
            pltpu.VMEM((RING, 2, tall, wide), jnp.bfloat16),
            dma((2, RING, RING, 2)),
            dma((2, RING, RING, 2)),
            dma((RING, 2)),
            dma((RING, 2)),
            dma((RING,)),
            dma((RING,)),
            dma,
        ],
        compiler_params=pltpu.CompilerParams(
            collective_id=4, has_side_effects=True, vmem_limit_bytes=48 * 2**20
        ),
        cost_estimate=pl.CostEstimate(
            flops=2 * tall * wide * tall * 8, bytes_accessed=4 * tall * wide * 4, transcendentals=0
        ),
    )(rounded, start, mix)


SLATER = (3.0 / 3.141592653589793) ** (1.0 / 3.0)


def potential_factor(values):
    return -SLATER * (values * values + 1.0) ** (1.0 / 6.0)


def body(
    basis_values,
    quad_weights,
    point_counts,
    basis_tiles,
    density,
    core_matrix,
    map_shift,
    map_scale,
    branch_flags,
):
    row_count = lax.axis_size("row")
    col_count = lax.axis_size("col")
    devices_all = row_count * col_count
    row_index = lax.axis_index("row")
    col_index = lax.axis_index("col")
    local_rows, local_cols = density.shape
    band_rows = local_rows // TILE
    band_cols = local_cols // TILE
    per_device = basis_values.shape[0]
    batch_total = basis_tiles.shape[0]
    points = basis_values.shape[1]
    width = basis_values.shape[2]
    blocks = width // TILE
    block_span = band_rows * row_count // blocks
    slots_row = max(1, band_rows // block_span)
    slots_col = max(1, band_cols // block_span)
    first_row = row_index * band_rows // block_span
    first_col = col_index * band_cols // block_span
    wanted_rows = jnp.take(basis_tiles, first_row + jnp.arange(slots_row, dtype=jnp.int32), axis=1)
    wanted_cols = jnp.take(basis_tiles, first_col + jnp.arange(slots_col, dtype=jnp.int32), axis=1)
    owned = (wanted_rows // band_rows == row_index)[:, :, None] & (
        wanted_cols // band_cols == col_index
    )[:, None, :]
    local_row = jnp.clip(wanted_rows - row_index * band_rows, 0, band_rows - 1)
    local_col = jnp.clip(wanted_cols - col_index * band_cols, 0, band_cols - 1)
    tile_grid = density.reshape(band_rows, TILE, band_cols, TILE).transpose(0, 2, 1, 3)
    outgoing = tile_grid[local_row[:, :, None], local_col[:, None, :]]
    outgoing = jnp.where(owned[:, :, :, None, None], outgoing, jnp.zeros((), jnp.bfloat16))
    outgoing = outgoing.reshape(devices_all, per_device, slots_row, slots_col, TILE, TILE)
    arrived = lax.all_to_all(outgoing, ("row", "col"), split_axis=0, concat_axis=0, tiled=True)
    my_start = (row_index * col_count + col_index) * per_device
    my_tiles = lax.dynamic_slice_in_dim(basis_tiles, my_start, per_device, 0)
    owner_row = my_tiles // band_rows
    owner_col = my_tiles // band_cols
    source = owner_row[:, :, None] * col_count + owner_col[:, None, :]
    block_ids = jnp.arange(blocks, dtype=jnp.int32)[None, :]
    slot_row = block_ids - owner_row * band_rows // block_span
    slot_col = block_ids - owner_col * band_cols // block_span
    batch_slot = jnp.arange(per_device, dtype=jnp.int32)[:, None, None]
    gathered = arrived[source, batch_slot, slot_row[:, :, None], slot_col[:, None, :]]
    submatrix = gathered.transpose(0, 1, 3, 2, 4).reshape(per_device, width, width)
    point_ids = jnp.arange(points, dtype=jnp.int32)
    values = basis_values[0]
    mixed = jnp.dot(values, submatrix[0], preferred_element_type=jnp.float32)
    local_density = jnp.sum(mixed * values.astype(jnp.float32), axis=1)
    live = point_ids < point_counts[0]
    local_density = jnp.where(live, local_density, jnp.float32(0.0))
    factor = jnp.where(live, quad_weights[0] * potential_factor(local_density), jnp.float32(0.0))
    weighted = (factor[:, None] * values).astype(jnp.bfloat16)
    contributions = [jnp.dot(values.T, weighted, preferred_element_type=jnp.float32)]
    densities = [local_density]
    block_tiles = (
        jnp.stack(contributions)
        .reshape(per_device, blocks, TILE, blocks, TILE)
        .transpose(0, 1, 3, 2, 4)
    )
    returning = jnp.zeros((devices_all, per_device, slots_row, slots_col, TILE, TILE), jnp.float32)
    returning = returning.at[source, batch_slot, slot_row[:, :, None], slot_col[:, None, :]].set(
        block_tiles
    )
    landed = lax.all_to_all(returning, ("row", "col"), split_axis=0, concat_axis=0, tiled=True)
    landed = landed.reshape(batch_total, slots_row, slots_col, TILE, TILE)
    landed = jnp.where(owned[:, :, :, None, None], landed, jnp.float32(0.0))
    row_target = local_row[:, :, None]
    col_target = local_col[:, None, :]
    summed = (
        jnp.zeros((band_rows, band_cols, TILE, TILE), jnp.float32)
        .at[row_target, col_target]
        .add(landed)
    )
    potential = summed.transpose(0, 2, 1, 3).reshape(local_rows, local_cols)
    global_rows = row_index * local_rows + jnp.arange(local_rows, dtype=jnp.int32)
    global_cols = col_index * local_cols + jnp.arange(local_cols, dtype=jnp.int32)
    identity = (global_rows[:, None] == global_cols[None, :]).astype(jnp.float32)
    start = map_shift[0] * identity + map_scale[0] * (core_matrix + potential)
    rounded = start.astype(jnp.bfloat16)
    keep = branch_flags[0] == 0
    mix = jnp.stack([jnp.where(keep, 1.0, -1.0), jnp.where(keep, 0.0, 2.0)]).astype(jnp.float32)
    purified = squared(rounded, start, mix)
    return (jnp.stack(densities), potential, purified)


def solution(mesh):
    placed = (
        P(("row", "col"), None, None),
        P(("row", "col"), None),
        P(("row", "col")),
        P(),
        P("row", "col"),
        P("row", "col"),
        P(),
        P(),
        P(),
    )
    return jax.shard_map(
        body,
        mesh=mesh,
        in_specs=placed,
        out_specs=(P(("row", "col"), None), P("row", "col"), P("row", "col")),
        check_vma=False,
    )
```

```python
import jax
import jax.numpy as jnp
from jax import lax
from jax.experimental import pallas as pl
from jax.experimental.pallas import tpu as pltpu
from jax.sharding import PartitionSpec as P

MESH = pl.DeviceIdType.MESH
TILE = 128
PART = TILE // 2
BLK = 8
BS = 6
RING = 4
COLS = 16
DEVICES = 128
STRIDE = 37


def turn(value, step):
    return lax.rem(value + (step % RING), RING)


def square_kernel(
    own_ref, start_ref, mix_ref, out_ref, rows_ref, cols_ref, row_send, row_recv, col_send, col_recv, core_send, core_recv, own_sem
):
    row, col = lax.axis_index("row"), lax.axis_index("col")
    z, core = row // 2, lax.rem(row, 2)
    x, y = col // RING, lax.rem(col, RING)
    tall, wide = own_ref.shape
    half = tall // 2
    quarter = half // 2

    def device(axis, step):
        if axis == "x":
            return (row, turn(x, step) * RING + y)
        if axis == "y":
            return (row, x * RING + turn(y, step))
        if axis == "z":
            return (turn(z, step) * 2 + core, col)
        return (z * 2 + 1 - core, col)

    def hop(place):
        position, part = place
        if position == 3:
            return 1, 0
        if position == 1:
            return -1, 0
        return (1, 3) if part == 0 else (-1, 1)

    def row_block(side, dx, dy):
        if dx == 0 and dy == 0:
            return own_ref.at[pl.ds(side * half, half)]
        return rows_ref.at[side, dx, dy]

    def row_copy(side, dx, dy, part=0):
        first, second = (dx, dy) if side == 0 else (dy, dx)
        axes = ("x", "y") if side == 0 else ("y", "x")
        place = second if second else first
        axis = axes[1] if second else axes[0]
        step, source = hop((place, part))
        origin = (first, source) if second else (source, 0)
        sx, sy = origin if side == 0 else origin[::-1]
        src, dst = row_block(side, sx, sy), rows_ref.at[side, dx, dy]
        if place == 2:
            cut = pl.ds(part * quarter, quarter)
            src, dst = src.at[cut], dst.at[cut]
        return pltpu.make_async_remote_copy(
            src_ref=src,
            dst_ref=dst,
            send_sem=row_send.at[side, dx, dy, part],
            recv_sem=row_recv.at[side, dx, dy, part],
            device_id=device(axis, step),
            device_id_type=MESH,
        )

    def col_copy(dz, part=0):
        step, source = hop((dz, part))
        slot = turn(z, source)
        src = own_ref if source == 0 else cols_ref.at[slot, core]
        dst = cols_ref.at[slot, core]
        if dz == 2:
            cut = pl.ds(part * half, half)
            src, dst = src.at[cut], dst.at[cut]
        return pltpu.make_async_remote_copy(
            src_ref=src,
            dst_ref=dst,
            send_sem=col_send.at[dz, part],
            recv_sem=col_recv.at[dz, part],
            device_id=device("z", step),
            device_id_type=MESH,
        )

    def core_copy(dz):
        slot = turn(z, dz)
        return pltpu.make_async_remote_copy(
            src_ref=own_ref if dz == 0 else cols_ref.at[slot, core],
            dst_ref=cols_ref.at[slot, core],
            send_sem=core_send.at[dz],
            recv_sem=core_recv.at[dz],
            device_id=device("core", 1),
            device_id_type=MESH,
        )

    def row_pair(side, first, second):
        return (first, second) if side == 0 else (second, first)

    barrier = pltpu.get_barrier_semaphore()
    partners = [device(a, s) for a in ("x", "y", "z") for s in (1, -1)] + [device("core", 1)]
    for partner in partners:
        pl.semaphore_signal(barrier, inc=1, device_id=partner, device_id_type=MESH)
    pl.semaphore_wait(barrier, len(partners))

    started = []

    def go(copy):
        copy.start()
        started.append(copy)

    for place in (3, 1):
        for side in (0, 1):
            go(row_copy(side, *row_pair(side, place, 0)))
    for place in (3, 1):
        go(col_copy(place))
    go(core_copy(0))
    for place in (3, 1):
        for side in (0, 1):
            go(row_copy(side, *row_pair(side, 0, place)))
    mine = pltpu.make_async_copy(own_ref, cols_ref.at[z, core], own_sem)
    mine.start()

    for place, part in ((3, 0), (1, 1)):
        for side in (0, 1):
            row_copy(side, *row_pair(side, place, 0)).wait_recv()
            go(row_copy(side, *row_pair(side, 2, 0), part))
        for side in (0, 1):
            for second in (3, 1):
                go(row_copy(side, *row_pair(side, place, second)))
        col_copy(place).wait_recv()
        go(col_copy(2, part))
        go(core_copy(place))
    for side in (0, 1):
        for part in (0, 1):
            row_copy(side, *row_pair(side, 2, 0), part).wait_recv()
        for second in (3, 1):
            go(row_copy(side, *row_pair(side, 2, second)))
    for part in (0, 1):
        col_copy(2, part).wait_recv()
    go(core_copy(2))

    def second_ring(first):
        for place, part in ((3, 0), (1, 1)):
            for side in (0, 1):
                row_copy(side, *row_pair(side, first, place)).wait_recv()
                go(row_copy(side, *row_pair(side, first, 2), part))

    def multiply(side, dx, dy):
        index = turn(x, dx) * RING + turn(y, dy)
        owner, cut = index // 2, lax.rem(index, 2)
        factor = cols_ref[owner // 2, lax.rem(owner, 2), pl.ds(pl.multiple_of(cut * wide, wide), wide), :]
        product = jnp.dot(row_block(side, dx, dy)[...], factor, preferred_element_type=jnp.float32)
        spot = pl.ds(side * half, half)
        if dx == 0 and dy == 0:
            out_ref[spot, :] = product
        else:
            out_ref[spot, :] += product

    second_ring(0)
    mine.wait()
    for dz in range(RING):
        core_copy(dz).wait_recv()
    for side in (0, 1):
        for first in range(RING):
            multiply(side, *row_pair(side, first, 0))
        for place in (3, 1):
            multiply(side, *row_pair(side, 0, place))
    for first in (3, 1, 2):
        second_ring(first)
        for side in (0, 1):
            for place in (3, 1):
                multiply(side, *row_pair(side, first, place))
    for first in (0, 3, 1, 2):
        for side in (0, 1):
            for part in (0, 1):
                row_copy(side, *row_pair(side, first, 2), part).wait_recv()
            multiply(side, *row_pair(side, first, 2))
    out_ref[...] = mix_ref[0] * out_ref[...] + mix_ref[1] * start_ref[...]
    for copy in started:
        copy.wait_send()


def squared(rounded, start, mix):
    tall, wide = rounded.shape
    vmem = pl.BlockSpec(memory_space=pltpu.VMEM)
    dma = pltpu.SemaphoreType.DMA
    return pl.pallas_call(
        square_kernel,
        name="square_kernel",
        out_shape=jax.ShapeDtypeStruct((tall, wide), jnp.float32),
        in_specs=[vmem, vmem, pl.BlockSpec(memory_space=pltpu.SMEM)],
        out_specs=vmem,
        scratch_shapes=[
            pltpu.VMEM((2, RING, RING, tall // 2, wide), jnp.bfloat16),
            pltpu.VMEM((RING, 2, tall, wide), jnp.bfloat16),
            dma((2, RING, RING, 2)),
            dma((2, RING, RING, 2)),
            dma((RING, 2)),
            dma((RING, 2)),
            dma((RING,)),
            dma((RING,)),
            dma,
        ],
        compiler_params=pltpu.CompilerParams(
            collective_id=4, has_side_effects=True, vmem_limit_bytes=48 * 2**20
        ),
        cost_estimate=pl.CostEstimate(
            flops=2 * tall * wide * tall * 8, bytes_accessed=4 * tall * wide * 4, transcendentals=0
        ),
    )(rounded, start, mix)


def device_at(index):
    return index // COLS, lax.rem(index, COLS)


def offset_device(row, col, step):
    z, core = row // 2, lax.rem(row, 2)
    x, y = col // RING, lax.rem(col, RING)
    dx, dy = step // 32, lax.rem(step // 8, RING)
    dz, dcore = lax.rem(step // 2, RING), lax.rem(step, 2)
    there = lax.rem(z + dz, RING) * 2 + lax.rem(core + dcore, 2)
    return there, lax.rem(x + dx, RING) * RING + lax.rem(y + dy, RING)


def spread(step):
    return lax.rem(step * STRIDE, DEVICES)


def greet_all(row, col):
    barrier = pltpu.get_barrier_semaphore()

    @pl.loop(1, DEVICES)
    def _(step):
        pl.semaphore_signal(barrier, inc=1, device_id=offset_device(row, col, step), device_id_type=MESH)

    pl.semaphore_wait(barrier, DEVICES - 1)


def tiles_in_kernel(
    tiles_ref, dens_ref, sub_ref, both_ref, out_ref, pair_send, pair_recv, own_sem, send_sem, recv_sem
):
    row, col = lax.axis_index("row"), lax.axis_index("col")
    slot, side = col // 2, lax.rem(col, 2)
    other = 1 - side
    greet_all(row, col)
    partner = (row, slot * 2 + other)
    pairs, mines = [], []
    for tile in range(BS // 2):
        cut = pl.ds(tile * TILE, TILE)
        spot = both_ref.at[pl.ds((side * (BS // 2) + tile) * BS, BS)]
        pairs.append(
            pltpu.make_async_remote_copy(
                src_ref=dens_ref.at[:, pl.ds(pl.multiple_of(other * PART, PART), PART), cut],
                dst_ref=spot,
                send_sem=pair_send.at[tile],
                recv_sem=pair_recv.at[tile],
                device_id=partner,
                device_id_type=MESH,
            )
        )
        mines.append(
            pltpu.make_async_copy(
                dens_ref.at[:, pl.ds(pl.multiple_of(side * PART, PART), PART), cut], spot, own_sem.at[tile]
            )
        )
    for copy in pairs + mines:
        copy.start()
    for copy in mines + pairs:
        copy.wait()
    spot_rows = pl.ds(pl.multiple_of(row * TILE + side * PART, PART), PART)
    spot_cols = pl.ds(pl.multiple_of(slot * TILE, TILE), TILE)

    def stage(target):
        batch = target[0] * COLS + target[1]
        tile_row = tiles_ref[batch * BLK + row] - row * BS
        tile_col = tiles_ref[batch * BLK + slot] - slot * BS
        out_ref[batch] = both_ref[jnp.clip(tile_col * BS + tile_row, 0, BS * BS - 1)]
        return batch

    @pl.loop(1, DEVICES)
    def _(count):
        target = offset_device(row, col, spread(count))
        batch = stage(target)
        pltpu.make_async_remote_copy(
            src_ref=out_ref.at[batch],
            dst_ref=sub_ref.at[spot_rows, spot_cols],
            send_sem=send_sem,
            recv_sem=recv_sem,
            device_id=target,
            device_id_type=MESH,
        ).start()

    batch = stage((row, col))
    pltpu.make_async_copy(out_ref.at[batch], sub_ref.at[spot_rows, spot_cols], recv_sem).start()
    pltpu.make_async_copy(sub_ref, sub_ref, recv_sem).wait()
    rest = out_ref.at[pl.ds(0, DEVICES - 1)]
    pltpu.make_async_copy(rest, rest, send_sem).wait()


def tiles_in(tiles, density):
    dma = pltpu.SemaphoreType.DMA
    tall, wide = density.shape
    return pl.pallas_call(
        tiles_in_kernel,
        name="tiles_in_kernel",
        out_shape=jax.ShapeDtypeStruct((BLK * TILE, BLK * TILE), jnp.bfloat16),
        in_specs=[pl.BlockSpec(memory_space=pltpu.SMEM), pl.BlockSpec(memory_space=pltpu.VMEM)],
        out_specs=pl.BlockSpec(memory_space=pltpu.VMEM),
        scratch_shapes=[
            pltpu.VMEM((BS * BS, PART, TILE), jnp.bfloat16),
            pltpu.VMEM((DEVICES, PART, TILE), jnp.bfloat16),
            dma((BS // 2,)),
            dma((BS // 2,)),
            dma((BS // 2,)),
            dma,
            dma,
        ],
        compiler_params=pltpu.CompilerParams(
            collective_id=1, has_side_effects=True, vmem_limit_bytes=32 * 2**20
        ),
        cost_estimate=pl.CostEstimate(flops=0, bytes_accessed=8 * 2**20, transcendentals=0),
    )(tiles.reshape(-1), density.reshape(BS, TILE, wide))


def tiles_back_kernel(
    block_ref,
    prev_ref,
    last_ref,
    map_ref,
    core_ref,
    xc_ref,
    start_ref,
    rounded_ref,
    landed_ref,
    sums_ref,
    give_ref,
    got_ref,
    pair_send,
    pair_recv,
    send_sem,
    recv_sem,
):
    row, col = lax.axis_index("row"), lax.axis_index("col")
    slot, side = col // 2, lax.rem(col, 2)
    other = 1 - side
    me = row * COLS + col
    greet_all(row, col)

    def piece(target):
        there_row, there_col = target
        first = there_row * TILE + lax.rem(there_col, 2) * PART
        return block_ref.at[
            pl.ds(pl.multiple_of(first, PART), PART),
            pl.ds(pl.multiple_of(there_col // 2 * TILE, TILE), TILE),
        ]

    @pl.loop(1, DEVICES)
    def _(count):
        target = offset_device(row, col, spread(count))
        pltpu.make_async_remote_copy(
            src_ref=piece(target),
            dst_ref=landed_ref.at[me],
            send_sem=send_sem,
            recv_sem=recv_sem,
            device_id=target,
            device_id_type=MESH,
        ).start()

    pltpu.make_async_copy(piece((row, col)), landed_ref.at[me], recv_sem).start()
    sums_ref[DEVICES] = jnp.zeros((PART, TILE), jnp.float32)
    pltpu.make_async_copy(landed_ref, landed_ref, recv_sem).wait()

    @pl.loop(0, DEVICES)
    def _(batch):
        sums_ref[batch] = sums_ref[prev_ref[batch]] + landed_ref[batch].astype(jnp.float32)

    def total(tile_row, half, tile):
        return sums_ref[last_ref[tile_row * BS + half * (BS // 2) + tile]]

    for tile_row in range(BS):
        for tile in range(BS // 2):
            cut = slice(tile * TILE, (tile + 1) * TILE)
            give_ref[tile_row, :, cut] = total(tile_row, other, tile).astype(give_ref.dtype)
    pair = pltpu.make_async_remote_copy(
        src_ref=give_ref,
        dst_ref=got_ref,
        send_sem=pair_send,
        recv_sem=pair_recv,
        device_id=(row, slot * 2 + other),
        device_id_type=MESH,
    )
    pair.start()

    wide = xc_ref.shape[1]

    def finish(first, value):
        spot = pl.ds(pl.multiple_of(first, PART), PART)
        xc_ref[spot, :] = value
        down = lax.broadcasted_iota(jnp.int32, value.shape, 0) + (row * BS * TILE + first)
        across = lax.broadcasted_iota(jnp.int32, value.shape, 1) + col * wide
        shift = jnp.where(down == across, map_ref[0], jnp.float32(0.0))
        start = shift + map_ref[1] * (core_ref[spot, :] + value)
        start_ref[spot, :] = start
        rounded_ref[spot, :] = start.astype(jnp.bfloat16)

    for tile_row in range(BS):
        mine = jnp.concatenate([total(tile_row, side, tile) for tile in range(BS // 2)], axis=1)
        finish(tile_row * TILE + side * PART, mine)
    pair.wait()
    for tile_row in range(BS):
        finish(tile_row * TILE + other * PART, got_ref[tile_row].astype(jnp.float32))
    rest = landed_ref.at[pl.ds(0, DEVICES - 1)]
    pltpu.make_async_copy(rest, rest, send_sem).wait()


def tiles_back(block, prev, last, mapping, core_matrix):
    dma = pltpu.SemaphoreType.DMA
    tall, wide = core_matrix.shape
    vmem = pl.BlockSpec(memory_space=pltpu.VMEM)
    smem = pl.BlockSpec(memory_space=pltpu.SMEM)
    return pl.pallas_call(
        tiles_back_kernel,
        name="tiles_back_kernel",
        out_shape=(
            jax.ShapeDtypeStruct((tall, wide), jnp.float32),
            jax.ShapeDtypeStruct((tall, wide), jnp.float32),
            jax.ShapeDtypeStruct((tall, wide), jnp.bfloat16),
        ),
        in_specs=[vmem, smem, smem, smem, vmem],
        out_specs=(vmem, vmem, vmem),
        scratch_shapes=[
            pltpu.VMEM((DEVICES, PART, TILE), jnp.bfloat16),
            pltpu.VMEM((DEVICES + 1, PART, TILE), jnp.float32),
            pltpu.VMEM((BS, PART, wide), jnp.bfloat16),
            pltpu.VMEM((BS, PART, wide), jnp.bfloat16),
            dma,
            dma,
            dma,
            dma,
        ],
        compiler_params=pltpu.CompilerParams(
            collective_id=2, has_side_effects=True, vmem_limit_bytes=40 * 2**20
        ),
        cost_estimate=pl.CostEstimate(flops=0, bytes_accessed=16 * 2**20, transcendentals=0),
    )(block, prev, last, mapping, core_matrix)


SLATER = (3.0 / 3.141592653589793) ** (1.0 / 3.0)


def potential_factor(values):
    return -SLATER * (values * values + 1.0) ** (1.0 / 6.0)


def body(
    basis_values,
    quad_weights,
    point_counts,
    basis_tiles,
    density,
    core_matrix,
    map_shift,
    map_scale,
    branch_flags,
):
    row, col = lax.axis_index("row"), lax.axis_index("col")
    points = basis_values.shape[1]
    submatrix = tiles_in(basis_tiles, density)

    batches = jnp.arange(DEVICES, dtype=jnp.int32)
    down = lax.dynamic_index_in_dim(basis_tiles, row, 1, keepdims=False) - row * BS
    across = lax.dynamic_index_in_dim(basis_tiles, col // 2, 1, keepdims=False) - col // 2 * BS
    key = down * BS + across
    earlier = (key[:, None] == key[None, :]) & (batches[None, :] < batches[:, None])
    prev = jnp.max(jnp.where(earlier, batches[None, :], -1), axis=1)
    prev = jnp.where(prev < 0, DEVICES, prev)
    hits = jnp.arange(BS * BS, dtype=jnp.int32)[:, None] == key[None, :]
    last = jnp.max(jnp.where(hits, batches[None, :], -1), axis=1)
    last = jnp.where(last < 0, DEVICES, last)

    point_ids = jnp.arange(points, dtype=jnp.int32)
    values = basis_values[0]
    mixed = jnp.dot(values, submatrix, preferred_element_type=jnp.float32)
    local_density = jnp.sum(mixed * values.astype(jnp.float32), axis=1)
    live = point_ids < point_counts[0]
    local_density = jnp.where(live, local_density, jnp.float32(0.0))
    factor = jnp.where(live, quad_weights[0] * potential_factor(local_density), jnp.float32(0.0))
    weighted = (factor[:, None] * values).astype(jnp.bfloat16)
    block = jnp.dot(values.T, weighted, preferred_element_type=jnp.float32).astype(jnp.bfloat16)
    mapping = jnp.concatenate([map_shift, map_scale])
    potential, start, rounded = tiles_back(block, prev, last, mapping, core_matrix)
    keep = branch_flags[0] == 0
    mix = jnp.stack([jnp.where(keep, 1.0, -1.0), jnp.where(keep, 0.0, 2.0)]).astype(jnp.float32)
    purified = squared(rounded, start, mix)
    return (local_density[None], potential, purified)


def solution(mesh):
    placed = (
        P(("row", "col"), None, None),
        P(("row", "col"), None),
        P(("row", "col")),
        P(),
        P("row", "col"),
        P("row", "col"),
        P(),
        P(),
        P(),
    )
    return jax.shard_map(
        body,
        mesh=mesh,
        in_specs=placed,
        out_specs=(P(("row", "col"), None), P("row", "col"), P("row", "col")),
        check_vma=False,
    )
```

```python
import jax
import jax.numpy as jnp
from jax import lax
from jax.experimental import pallas as pl
from jax.experimental.pallas import tpu as pltpu
from jax.sharding import PartitionSpec as P

MESH = pl.DeviceIdType.MESH
TILE = 128
PART = TILE // 2
BLK = 8
BS = 6
RING = 4
COLS = 16
DEVICES = 128
STRIDE = 37
SLATER = (3.0 / 3.141592653589793) ** (1.0 / 3.0)

def potential_factor(values):
    return -SLATER * (values * values + 1.0) ** (1.0 / 6.0)


def turn(value, step):
    return lax.rem(value + (step % RING), RING)


def offset_device(row, col, step):
    z, core = row // 2, lax.rem(row, 2)
    x, y = col // RING, lax.rem(col, RING)
    dx, dy = step // 32, lax.rem(step // 8, RING)
    dz, dcore = lax.rem(step // 2, RING), lax.rem(step, 2)
    there = lax.rem(z + dz, RING) * 2 + lax.rem(core + dcore, 2)
    return there, lax.rem(x + dx, RING) * RING + lax.rem(y + dy, RING)


CHUNK = 256
SLAB = 512


def greet_all(row, col):
    barrier = pltpu.get_barrier_semaphore()

    @pl.loop(1, DEVICES)
    def _(step):
        pl.semaphore_signal(barrier, inc=1, device_id=offset_device(row, col, step), device_id_type=MESH)

    pl.semaphore_wait(barrier, DEVICES - 1)


def square(
    row, col, own_ref, start_ref, scalar_ref, out_ref, rows_ref, cols_ref,
    row_send, row_recv, col_send, col_recv, core_send, core_recv, own_sem,
):
    z, core = row // 2, lax.rem(row, 2)
    x, y = col // RING, lax.rem(col, RING)
    tall, wide = own_ref.shape
    half = tall // 2
    quarter = half // 2

    def device(axis, step):
        if axis == "x":
            return (row, turn(x, step) * RING + y)
        if axis == "y":
            return (row, x * RING + turn(y, step))
        if axis == "z":
            return (turn(z, step) * 2 + core, col)
        return (z * 2 + 1 - core, col)

    def hop(place):
        position, part = place
        if position == 3:
            return 1, 0
        if position == 1:
            return -1, 0
        return (1, 3) if part == 0 else (-1, 1)

    def row_block(side, dx, dy):
        if dx == 0 and dy == 0:
            return own_ref.at[pl.ds(side * half, half)]
        return rows_ref.at[side, dx, dy]

    def row_copy(side, dx, dy, part=0):
        first, second = (dx, dy) if side == 0 else (dy, dx)
        axes = ("x", "y") if side == 0 else ("y", "x")
        place = second if second else first
        axis = axes[1] if second else axes[0]
        step, source = hop((place, part))
        origin = (first, source) if second else (source, 0)
        sx, sy = origin if side == 0 else origin[::-1]
        src, dst = row_block(side, sx, sy), rows_ref.at[side, dx, dy]
        if place == 2:
            cut = pl.ds(part * quarter, quarter)
            src, dst = src.at[cut], dst.at[cut]
        return pltpu.make_async_remote_copy(
            src_ref=src,
            dst_ref=dst,
            send_sem=row_send.at[side, dx, dy, part],
            recv_sem=row_recv.at[side, dx, dy, part],
            device_id=device(axis, step),
            device_id_type=MESH,
        )

    def col_copy(dz, part=0):
        step, source = hop((dz, part))
        slot = turn(z, source)
        src = own_ref if source == 0 else cols_ref.at[slot, core]
        dst = cols_ref.at[slot, core]
        if dz == 2:
            cut = pl.ds(part * half, half)
            src, dst = src.at[cut], dst.at[cut]
        return pltpu.make_async_remote_copy(
            src_ref=src,
            dst_ref=dst,
            send_sem=col_send.at[dz, part],
            recv_sem=col_recv.at[dz, part],
            device_id=device("z", step),
            device_id_type=MESH,
        )

    def core_copy(dz):
        slot = turn(z, dz)
        return pltpu.make_async_remote_copy(
            src_ref=own_ref if dz == 0 else cols_ref.at[slot, core],
            dst_ref=cols_ref.at[slot, core],
            send_sem=core_send.at[dz],
            recv_sem=core_recv.at[dz],
            device_id=device("core", 1),
            device_id_type=MESH,
        )

    def row_pair(side, first, second):
        return (first, second) if side == 0 else (second, first)

    started = []

    def go(copy):
        copy.start()
        started.append(copy)

    for place in (3, 1):
        for side in (0, 1):
            go(row_copy(side, *row_pair(side, place, 0)))
    for place in (3, 1):
        go(col_copy(place))
    go(core_copy(0))
    for place in (3, 1):
        for side in (0, 1):
            go(row_copy(side, *row_pair(side, 0, place)))
    mine = pltpu.make_async_copy(own_ref, cols_ref.at[z, core], own_sem)
    mine.start()

    for place, part in ((3, 0), (1, 1)):
        for side in (0, 1):
            row_copy(side, *row_pair(side, place, 0)).wait_recv()
            go(row_copy(side, *row_pair(side, 2, 0), part))
        for side in (0, 1):
            for second in (3, 1):
                go(row_copy(side, *row_pair(side, place, second)))
        col_copy(place).wait_recv()
        go(col_copy(2, part))
        go(core_copy(place))
    for side in (0, 1):
        for part in (0, 1):
            row_copy(side, *row_pair(side, 2, 0), part).wait_recv()
        for second in (3, 1):
            go(row_copy(side, *row_pair(side, 2, second)))
    for part in (0, 1):
        col_copy(2, part).wait_recv()
    go(core_copy(2))

    def second_ring(first):
        for place, part in ((3, 0), (1, 1)):
            for side in (0, 1):
                row_copy(side, *row_pair(side, first, place)).wait_recv()
                go(row_copy(side, *row_pair(side, first, 2), part))

    def multiply(side, dx, dy):
        index = turn(x, dx) * RING + turn(y, dy)
        owner, cut = index // 2, lax.rem(index, 2)
        factor = cols_ref[owner // 2, lax.rem(owner, 2), pl.ds(pl.multiple_of(cut * wide, wide), wide), :]
        product = jnp.dot(row_block(side, dx, dy)[...], factor, preferred_element_type=jnp.float32)
        spot = pl.ds(side * half, half)
        if dx == 0 and dy == 0:
            out_ref[spot, :] = product
        else:
            out_ref[spot, :] += product

    second_ring(0)
    mine.wait()
    for dz in range(RING):
        core_copy(dz).wait_recv()
    for side in (0, 1):
        for first in range(RING):
            multiply(side, *row_pair(side, first, 0))
        for place in (3, 1):
            multiply(side, *row_pair(side, 0, place))
    for first in (3, 1, 2):
        second_ring(first)
        for side in (0, 1):
            for place in (3, 1):
                multiply(side, *row_pair(side, first, place))
    for first in (0, 3, 1, 2):
        for side in (0, 1):
            for part in (0, 1):
                row_copy(side, *row_pair(side, first, 2), part).wait_recv()
            multiply(side, *row_pair(side, first, 2))
    out_ref[...] = scalar_ref[2] * out_ref[...] + scalar_ref[3] * start_ref[...]
    for copy in started:
        copy.wait_send()

def whole_kernel(
    tiles_ref,
    prev_ref,
    last_ref,
    scalar_ref,
    count_ref,
    weights_ref,
    dens_ref,
    basis_hbm,
    core_hbm,
    rho_ref,
    xc_ref,
    out_ref,
    basis_ref,
    core_ref,
    turned_ref,
    scaled_ref,
    both_ref,
    stage_ref,
    sub_ref,
    block_ref,
    landed_ref,
    sums_ref,
    give_ref,
    got_ref,
    start_ref,
    rounded_ref,
    rows_ref,
    cols_ref,
    load_sem,
    in_send,
    in_recv,
    in_own,
    back_send,
    back_recv,
    all_send,
    all_recv,
    row_send,
    row_recv,
    col_send,
    col_recv,
    core_send,
    core_recv,
    own_sem,
):
    row, col = lax.axis_index("row"), lax.axis_index("col")
    slot, side = col // 2, lax.rem(col, 2)
    other = 1 - side
    me = row * COLS + col
    partner = (row, slot * 2 + other)
    load_basis = pltpu.make_async_copy(basis_hbm, basis_ref, load_sem.at[0])
    load_core = pltpu.make_async_copy(core_hbm, core_ref, load_sem.at[1])
    load_basis.start()
    load_core.start()
    greet_all(row, col)

    pairs, mines = [], []
    for tile in range(BS // 2):
        cut = pl.ds(tile * TILE, TILE)
        spot = both_ref.at[pl.ds((side * (BS // 2) + tile) * BS, BS)]
        pairs.append(
            pltpu.make_async_remote_copy(
                src_ref=dens_ref.at[:, pl.ds(pl.multiple_of(other * PART, PART), PART), cut],
                dst_ref=spot,
                send_sem=in_send.at[tile],
                recv_sem=in_recv.at[tile],
                device_id=partner,
                device_id_type=MESH,
            )
        )
        mines.append(
            pltpu.make_async_copy(
                dens_ref.at[:, pl.ds(pl.multiple_of(side * PART, PART), PART), cut], spot, in_own.at[tile]
            )
        )
    for copy in pairs + mines:
        copy.start()
    for copy in mines + pairs:
        copy.wait()

    spot_rows = pl.ds(pl.multiple_of(row * TILE + side * PART, PART), PART)
    spot_cols = pl.ds(pl.multiple_of(slot * TILE, TILE), TILE)

    def stage(target):
        batch = target[0] * COLS + target[1]
        tile_row = tiles_ref[batch * BLK + row] - row * BS
        tile_col = tiles_ref[batch * BLK + slot] - slot * BS
        stage_ref[batch] = both_ref[jnp.clip(tile_col * BS + tile_row, 0, BS * BS - 1)]
        return batch

    @pl.loop(1, DEVICES)
    def _(count):
        target = offset_device(row, col, lax.rem(count * STRIDE, DEVICES))
        batch = stage(target)
        pltpu.make_async_remote_copy(
            src_ref=stage_ref.at[batch],
            dst_ref=sub_ref.at[spot_rows, spot_cols],
            send_sem=all_send.at[0],
            recv_sem=all_recv.at[0],
            device_id=target,
            device_id_type=MESH,
        ).start()

    stage((row, col))
    pltpu.make_async_copy(stage_ref.at[me], sub_ref.at[spot_rows, spot_cols], all_recv.at[0]).start()

    points, width = basis_ref.shape
    load_basis.wait()

    @pl.loop(0, points // CHUNK)
    def _(step):
        first = pl.multiple_of(step * CHUNK, CHUNK)
        turned_ref[:, pl.ds(first, CHUNK)] = basis_ref[pl.ds(first, CHUNK), :].T

    pltpu.make_async_copy(sub_ref, sub_ref, all_recv.at[0]).wait()

    @pl.loop(0, points // CHUNK)
    def _(step):
        cut = pl.ds(pl.multiple_of(step * CHUNK, CHUNK), CHUNK)
        mixed = jnp.dot(sub_ref[...], turned_ref[:, cut], preferred_element_type=jnp.float32)
        values = turned_ref[:, cut].astype(jnp.float32)
        density = jnp.sum(mixed * values, axis=0, keepdims=True)
        live = lax.broadcasted_iota(jnp.int32, density.shape, 1) + step * CHUNK < count_ref[0]
        density = jnp.where(live, density, jnp.float32(0.0))
        rho_ref[:, cut] = density
        factor = jnp.where(live, weights_ref[:, cut] * potential_factor(density), jnp.float32(0.0))
        scaled_ref[:, cut] = (factor * values).astype(jnp.bfloat16)

    @pl.loop(0, width // SLAB)
    def _(step):
        spot = pl.ds(pl.multiple_of(step * SLAB, SLAB), SLAB)
        block_ref[spot, :] = lax.dot_general(
            turned_ref[spot, :], scaled_ref[...], (((1,), (1,)), ((), ())), preferred_element_type=jnp.float32
        ).astype(jnp.bfloat16)

    def piece(target):
        there_row, there_col = target
        first = there_row * TILE + lax.rem(there_col, 2) * PART
        return block_ref.at[
            pl.ds(pl.multiple_of(first, PART), PART),
            pl.ds(pl.multiple_of(there_col // 2 * TILE, TILE), TILE),
        ]

    @pl.loop(1, DEVICES)
    def _(count):
        target = offset_device(row, col, lax.rem(count * STRIDE, DEVICES))
        pltpu.make_async_remote_copy(
            src_ref=piece(target),
            dst_ref=landed_ref.at[me],
            send_sem=all_send.at[1],
            recv_sem=all_recv.at[1],
            device_id=target,
            device_id_type=MESH,
        ).start()

    pltpu.make_async_copy(piece((row, col)), landed_ref.at[me], all_recv.at[1]).start()
    sums_ref[DEVICES] = jnp.zeros((PART, TILE), jnp.float32)
    rest = stage_ref.at[pl.ds(0, DEVICES - 1)]
    pltpu.make_async_copy(rest, rest, all_send.at[0]).wait()
    load_core.wait()
    pltpu.make_async_copy(landed_ref, landed_ref, all_recv.at[1]).wait()

    @pl.loop(0, DEVICES)
    def _(batch):
        sums_ref[batch] = sums_ref[prev_ref[batch]] + landed_ref[batch].astype(jnp.float32)

    def total(tile_row, half, tile):
        return sums_ref[last_ref[tile_row * BS + half * (BS // 2) + tile]]

    for tile_row in range(BS):
        for tile in range(BS // 2):
            cut = slice(tile * TILE, (tile + 1) * TILE)
            give_ref[tile_row, :, cut] = total(tile_row, other, tile).astype(give_ref.dtype)
    pair = pltpu.make_async_remote_copy(
        src_ref=give_ref,
        dst_ref=got_ref,
        send_sem=back_send,
        recv_sem=back_recv,
        device_id=partner,
        device_id_type=MESH,
    )
    pair.start()

    def finish(first, value):
        spot = pl.ds(pl.multiple_of(first, PART), PART)
        xc_ref[spot, :] = value
        down = lax.broadcasted_iota(jnp.int32, value.shape, 0) + (row * BS * TILE + first)
        across = lax.broadcasted_iota(jnp.int32, value.shape, 1) + col * xc_ref.shape[1]
        shift = jnp.where(down == across, scalar_ref[0], jnp.float32(0.0))
        start = shift + scalar_ref[1] * (core_ref[spot, :] + value)
        start_ref[spot, :] = start
        rounded_ref[spot, :] = start.astype(jnp.bfloat16)

    for tile_row in range(BS):
        mine = jnp.concatenate([total(tile_row, side, tile) for tile in range(BS // 2)], axis=1)
        finish(tile_row * TILE + side * PART, mine)
    pair.wait()
    for tile_row in range(BS):
        finish(tile_row * TILE + other * PART, got_ref[tile_row].astype(jnp.float32))

    square(
        row, col, rounded_ref, start_ref, scalar_ref, out_ref, rows_ref, cols_ref,
        row_send, row_recv, col_send, col_recv, core_send, core_recv, own_sem,
    )
    rest = landed_ref.at[pl.ds(0, DEVICES - 1)]
    pltpu.make_async_copy(rest, rest, all_send.at[1]).wait()


def whole(tiles, prev, last, scalars, count, weights, density, basis, core_matrix):
    dma = pltpu.SemaphoreType.DMA
    tall, wide = core_matrix.shape
    points, width = basis.shape
    vmem = pl.BlockSpec(memory_space=pltpu.VMEM)
    smem = pl.BlockSpec(memory_space=pltpu.SMEM)
    hbm = pl.BlockSpec(memory_space=pl.ANY)
    bf16, f32 = jnp.bfloat16, jnp.float32
    return pl.pallas_call(
        whole_kernel,
        name="whole_kernel",
        out_shape=(
            jax.ShapeDtypeStruct((1, points), f32),
            jax.ShapeDtypeStruct((tall, wide), f32),
            jax.ShapeDtypeStruct((tall, wide), f32),
        ),
        in_specs=[smem, smem, smem, smem, smem, vmem, vmem, hbm, hbm],
        out_specs=(vmem, vmem, vmem),
        scratch_shapes=[
            pltpu.VMEM((points, width), bf16),
            pltpu.VMEM((tall, wide), f32),
            pltpu.VMEM((width, points), bf16),
            pltpu.VMEM((width, points), bf16),
            pltpu.VMEM((BS * BS, PART, TILE), bf16),
            pltpu.VMEM((DEVICES, PART, TILE), bf16),
            pltpu.VMEM((width, width), bf16),
            pltpu.VMEM((width, width), bf16),
            pltpu.VMEM((DEVICES, PART, TILE), bf16),
            pltpu.VMEM((DEVICES + 1, PART, TILE), f32),
            pltpu.VMEM((BS, PART, wide), bf16),
            pltpu.VMEM((BS, PART, wide), bf16),
            pltpu.VMEM((tall, wide), f32),
            pltpu.VMEM((tall, wide), bf16),
            pltpu.VMEM((2, RING, RING, tall // 2, wide), bf16),
            pltpu.VMEM((RING, 2, tall, wide), bf16),
            dma((2,)),
            dma((BS // 2,)),
            dma((BS // 2,)),
            dma((BS // 2,)),
            dma,
            dma,
            dma((2,)),
            dma((2,)),
            dma((2, RING, RING, 2)),
            dma((2, RING, RING, 2)),
            dma((RING, 2)),
            dma((RING, 2)),
            dma((RING,)),
            dma((RING,)),
            dma,
        ],
        compiler_params=pltpu.CompilerParams(
            collective_id=1, has_side_effects=True, vmem_limit_bytes=56 * 2**20
        ),
        cost_estimate=pl.CostEstimate(
            flops=4 * points * width * width + 2 * tall * wide * tall * 8, bytes_accessed=16 * 2**20, transcendentals=0
        ),
    )(tiles.reshape(-1), prev, last, scalars, count, weights, density.reshape(BS, TILE, wide), basis, core_matrix)


def body(
    basis_values,
    quad_weights,
    point_counts,
    basis_tiles,
    density,
    core_matrix,
    map_shift,
    map_scale,
    branch_flags,
):
    row, col = lax.axis_index("row"), lax.axis_index("col")
    batches = jnp.arange(DEVICES, dtype=jnp.int32)
    down = lax.dynamic_index_in_dim(basis_tiles, row, 1, keepdims=False) - row * BS
    across = lax.dynamic_index_in_dim(basis_tiles, col // 2, 1, keepdims=False) - col // 2 * BS
    key = down * BS + across
    earlier = (key[:, None] == key[None, :]) & (batches[None, :] < batches[:, None])
    prev = jnp.max(jnp.where(earlier, batches[None, :], -1), axis=1)
    prev = jnp.where(prev < 0, DEVICES, prev)
    hits = jnp.arange(BS * BS, dtype=jnp.int32)[:, None] == key[None, :]
    last = jnp.max(jnp.where(hits, batches[None, :], -1), axis=1)
    last = jnp.where(last < 0, DEVICES, last)

    keep = branch_flags[0] == 0
    scalars = jnp.concatenate(
        [map_shift, map_scale, jnp.where(keep, 1.0, -1.0)[None], jnp.where(keep, 0.0, 2.0)[None]]
    ).astype(jnp.float32)
    local_density, potential, purified = whole(
        basis_tiles, prev, last, scalars, point_counts, quad_weights, density, basis_values[0], core_matrix
    )
    return (local_density, potential, purified)


def solution(mesh):
    placed = (
        P(("row", "col"), None, None),
        P(("row", "col"), None),
        P(("row", "col")),
        P(),
        P("row", "col"),
        P("row", "col"),
        P(),
        P(),
        P(),
    )
    return jax.shard_map(
        body,
        mesh=mesh,
        in_specs=placed,
        out_specs=(P(("row", "col"), None), P("row", "col"), P("row", "col")),
        check_vma=False,
    )
```

```python
import jax
import jax.numpy as jnp
from jax import lax
from jax.experimental import pallas as pl
from jax.experimental.pallas import tpu as pltpu
from jax.sharding import PartitionSpec as P

MESH = pl.DeviceIdType.MESH
TILE = 128
PART = TILE // 2
BLK = 8
BS = 6
RING = 4
COLS = 16
DEVICES = 128
STRIDE = 37
SLATER = (3.0 / 3.141592653589793) ** (1.0 / 3.0)

def potential_factor(values):
    return -SLATER * (values * values + 1.0) ** (1.0 / 6.0)


def turn(value, step):
    return lax.rem(value + (step % RING), RING)


def offset_device(row, col, step):
    z, core = row // 2, lax.rem(row, 2)
    x, y = col // RING, lax.rem(col, RING)
    dx, dy = step // 32, lax.rem(step // 8, RING)
    dz, dcore = lax.rem(step // 2, RING), lax.rem(step, 2)
    there = lax.rem(z + dz, RING) * 2 + lax.rem(core + dcore, 2)
    return there, lax.rem(x + dx, RING) * RING + lax.rem(y + dy, RING)


CHUNK = 256
SLAB = 512


def greet_all(me):
    barrier = pltpu.get_barrier_semaphore()

    @pl.loop(1, DEVICES, unroll=8)
    def _(step):
        there = lax.rem(me + step, DEVICES)
        pl.semaphore_signal(
            barrier, inc=1, device_id=(there // COLS, lax.rem(there, COLS)), device_id_type=MESH
        )

    return barrier


def square(
    row, col, own_ref, start_ref, flag_ref, out_ref, rows_ref, cols_ref,
    row_send, row_recv, col_send, col_recv, core_send, core_recv, own_sem,
):
    z, core = row // 2, lax.rem(row, 2)
    x, y = col // RING, lax.rem(col, RING)
    tall, wide = own_ref.shape
    half = tall // 2
    quarter = half // 2

    def device(axis, step):
        if axis == "x":
            return (row, turn(x, step) * RING + y)
        if axis == "y":
            return (row, x * RING + turn(y, step))
        if axis == "z":
            return (turn(z, step) * 2 + core, col)
        return (z * 2 + 1 - core, col)

    def hop(place):
        position, part = place
        if position == 3:
            return 1, 0
        if position == 1:
            return -1, 0
        return (1, 3) if part == 0 else (-1, 1)

    def row_block(side, dx, dy):
        if dx == 0 and dy == 0:
            return own_ref.at[pl.ds(side * half, half)]
        return rows_ref.at[side, dx, dy]

    def row_copy(side, dx, dy, part=0):
        first, second = (dx, dy) if side == 0 else (dy, dx)
        axes = ("x", "y") if side == 0 else ("y", "x")
        place = second if second else first
        axis = axes[1] if second else axes[0]
        step, source = hop((place, part))
        origin = (first, source) if second else (source, 0)
        sx, sy = origin if side == 0 else origin[::-1]
        src, dst = row_block(side, sx, sy), rows_ref.at[side, dx, dy]
        if place == 2:
            cut = pl.ds(part * quarter, quarter)
            src, dst = src.at[cut], dst.at[cut]
        return pltpu.make_async_remote_copy(
            src_ref=src,
            dst_ref=dst,
            send_sem=row_send.at[side, dx, dy, part],
            recv_sem=row_recv.at[side, dx, dy, part],
            device_id=device(axis, step),
            device_id_type=MESH,
        )

    def col_copy(dz, part=0):
        step, source = hop((dz, part))
        slot = turn(z, source)
        src = own_ref if source == 0 else cols_ref.at[slot, core]
        dst = cols_ref.at[slot, core]
        if dz == 2:
            cut = pl.ds(part * half, half)
            src, dst = src.at[cut], dst.at[cut]
        return pltpu.make_async_remote_copy(
            src_ref=src,
            dst_ref=dst,
            send_sem=col_send.at[dz, part],
            recv_sem=col_recv.at[dz, part],
            device_id=device("z", step),
            device_id_type=MESH,
        )

    def core_copy(dz):
        slot = turn(z, dz)
        return pltpu.make_async_remote_copy(
            src_ref=own_ref if dz == 0 else cols_ref.at[slot, core],
            dst_ref=cols_ref.at[slot, core],
            send_sem=core_send.at[dz],
            recv_sem=core_recv.at[dz],
            device_id=device("core", 1),
            device_id_type=MESH,
        )

    def row_pair(side, first, second):
        return (first, second) if side == 0 else (second, first)

    started = []

    def go(copy):
        copy.start()
        started.append(copy)

    for place in (3, 1):
        for side in (0, 1):
            go(row_copy(side, *row_pair(side, place, 0)))
    for place in (3, 1):
        go(col_copy(place))
    go(core_copy(0))
    for place in (3, 1):
        for side in (0, 1):
            go(row_copy(side, *row_pair(side, 0, place)))
    mine = pltpu.make_async_copy(own_ref, cols_ref.at[z, core], own_sem)
    mine.start()

    for place, part in ((3, 0), (1, 1)):
        for side in (0, 1):
            row_copy(side, *row_pair(side, place, 0)).wait_recv()
            go(row_copy(side, *row_pair(side, 2, 0), part))
        for side in (0, 1):
            for second in (3, 1):
                go(row_copy(side, *row_pair(side, place, second)))
        col_copy(place).wait_recv()
        go(col_copy(2, part))
        go(core_copy(place))
    for side in (0, 1):
        for part in (0, 1):
            row_copy(side, *row_pair(side, 2, 0), part).wait_recv()
        for second in (3, 1):
            go(row_copy(side, *row_pair(side, 2, second)))
    for part in (0, 1):
        col_copy(2, part).wait_recv()
    go(core_copy(2))

    def second_ring(first):
        for place, part in ((3, 0), (1, 1)):
            for side in (0, 1):
                row_copy(side, *row_pair(side, first, place)).wait_recv()
                go(row_copy(side, *row_pair(side, first, 2), part))

    def multiply(side, dx, dy):
        index = turn(x, dx) * RING + turn(y, dy)
        owner, cut = index // 2, lax.rem(index, 2)
        factor = cols_ref[owner // 2, lax.rem(owner, 2), pl.ds(pl.multiple_of(cut * wide, wide), wide), :]
        product = jnp.dot(row_block(side, dx, dy)[...], factor, preferred_element_type=jnp.float32)
        spot = pl.ds(side * half, half)
        if dx == 0 and dy == 0:
            out_ref[spot, :] = product
        else:
            out_ref[spot, :] += product

    second_ring(0)
    mine.wait()
    for dz in range(RING):
        core_copy(dz).wait_recv()
    for side in (0, 1):
        for first in range(RING):
            multiply(side, *row_pair(side, first, 0))
        for place in (3, 1):
            multiply(side, *row_pair(side, 0, place))
    for first in (3, 1, 2):
        second_ring(first)
        for side in (0, 1):
            for place in (3, 1):
                multiply(side, *row_pair(side, first, place))
    for first in (0, 3, 1, 2):
        for side in (0, 1):
            for part in (0, 1):
                row_copy(side, *row_pair(side, first, 2), part).wait_recv()
            multiply(side, *row_pair(side, first, 2))
    keep = flag_ref[0] == 0
    sign = jnp.where(keep, 1.0, -1.0)
    twice = jnp.where(keep, 0.0, 2.0)
    out_ref[...] = sign * out_ref[...] + twice * start_ref[...]
    for copy in started:
        copy.wait_send()

def whole_kernel(
    shift_ref,
    scale_ref,
    flag_ref,
    count_ref,
    weights_ref,
    tiles_hbm,
    dens_ref,
    basis_hbm,
    core_hbm,
    rho_hbm,
    xc_hbm,
    out_hbm,
    tiles_ref,
    tiles_vec,
    chain_vec,
    chain_ref,
    rho_ref,
    xc_ref,
    out_ref,
    basis_ref,
    core_ref,
    turned_ref,
    scaled_ref,
    both_ref,
    stage_ref,
    sub_ref,
    block_ref,
    landed_ref,
    sums_ref,
    give_ref,
    got_ref,
    start_ref,
    rounded_ref,
    rows_ref,
    cols_ref,
    load_sem,
    in_send,
    in_recv,
    in_own,
    back_send,
    back_recv,
    all_send,
    all_recv,
    row_send,
    row_recv,
    col_send,
    col_recv,
    core_send,
    core_recv,
    own_sem,
):
    row, col = lax.axis_index("row"), lax.axis_index("col")
    slot, side = col // 2, lax.rem(col, 2)
    other = 1 - side
    me = row * COLS + col
    partner = (row, slot * 2 + other)
    load_basis = pltpu.make_async_copy(basis_hbm, basis_ref, load_sem.at[0])
    load_core = pltpu.make_async_copy(core_hbm, core_ref, load_sem.at[1])
    load_tiles = [
        pltpu.make_async_copy(tiles_hbm, tiles_ref, load_sem.at[2]),
        pltpu.make_async_copy(tiles_hbm, tiles_vec, load_sem.at[3]),
    ]
    for copy in load_tiles:
        copy.start()
    barrier = greet_all(me)
    for copy in load_tiles:
        copy.wait()

    pairs, mines = [], []
    for tile in range(BS // 2):
        cut = pl.ds(tile * TILE, TILE)
        spot = both_ref.at[pl.ds((side * (BS // 2) + tile) * BS, BS)]
        pairs.append(
            pltpu.make_async_remote_copy(
                src_ref=dens_ref.at[:, pl.ds(pl.multiple_of(other * PART, PART), PART), cut],
                dst_ref=spot,
                send_sem=in_send.at[tile],
                recv_sem=in_recv.at[tile],
                device_id=partner,
                device_id_type=MESH,
            )
        )
        mines.append(
            pltpu.make_async_copy(
                dens_ref.at[:, pl.ds(pl.multiple_of(side * PART, PART), PART), cut], spot, in_own.at[tile]
            )
        )
    for copy in mines:
        copy.start()
    pl.semaphore_wait(barrier, DEVICES - 1)
    for copy in pairs:
        copy.start()
    load_basis.start()
    load_core.start()
    for copy in mines + pairs:
        copy.wait()

    spot_rows = pl.ds(pl.multiple_of(row * TILE + side * PART, PART), PART)
    spot_cols = pl.ds(pl.multiple_of(slot * TILE, TILE), TILE)

    def stage(target):
        batch = target[0] * COLS + target[1]
        tile_row = tiles_ref[row, batch] - row * BS
        tile_col = tiles_ref[slot, batch] - slot * BS
        stage_ref[batch] = both_ref[jnp.clip(tile_col * BS + tile_row, 0, BS * BS - 1)]
        return batch

    @pl.loop(1, DEVICES)
    def _(count):
        target = offset_device(row, col, lax.rem(count * STRIDE, DEVICES))
        batch = stage(target)
        pltpu.make_async_remote_copy(
            src_ref=stage_ref.at[batch],
            dst_ref=sub_ref.at[spot_rows, spot_cols],
            send_sem=all_send.at[0],
            recv_sem=all_recv.at[0],
            device_id=target,
            device_id_type=MESH,
        ).start()

    stage((row, col))
    pltpu.make_async_copy(stage_ref.at[me], sub_ref.at[spot_rows, spot_cols], all_recv.at[0]).start()

    key = (tiles_vec[pl.ds(row, 1), :] - row * BS) * BS + tiles_vec[pl.ds(slot, 1), :] - slot * BS
    across = jnp.broadcast_to(key, (DEVICES, DEVICES))
    down = across.T
    batch_down = lax.broadcasted_iota(jnp.int32, across.shape, 0)
    batch_across = lax.broadcasted_iota(jnp.int32, across.shape, 1)
    earlier = (down == across) & (batch_down < batch_across)
    prev = jnp.max(jnp.where(earlier, batch_down, -1), axis=0, keepdims=True)
    last = jnp.max(jnp.where(down == batch_across, batch_down, -1), axis=0, keepdims=True)
    chain_vec[...] = jnp.zeros_like(chain_vec)
    chain_vec[0:1, :] = jnp.where(prev < 0, DEVICES, prev)
    chain_vec[1:2, :] = jnp.where(last < 0, DEVICES, last)
    load_chain = pltpu.make_async_copy(chain_vec, chain_ref, load_sem.at[4])
    load_chain.start()

    points, width = basis_ref.shape
    load_basis.wait()

    @pl.loop(0, points // CHUNK)
    def _(step):
        first = pl.multiple_of(step * CHUNK, CHUNK)
        turned_ref[:, pl.ds(first, CHUNK)] = basis_ref[pl.ds(first, CHUNK), :].T

    pltpu.make_async_copy(sub_ref, sub_ref, all_recv.at[0]).wait()

    @pl.loop(0, points // CHUNK)
    def _(step):
        cut = pl.ds(pl.multiple_of(step * CHUNK, CHUNK), CHUNK)
        mixed = jnp.dot(sub_ref[...], turned_ref[:, cut], preferred_element_type=jnp.float32)
        values = turned_ref[:, cut].astype(jnp.float32)
        density = jnp.sum(mixed * values, axis=0, keepdims=True)
        live = lax.broadcasted_iota(jnp.int32, density.shape, 1) + step * CHUNK < count_ref[0]
        density = jnp.where(live, density, jnp.float32(0.0))
        rho_ref[:, cut] = density
        factor = jnp.where(live, weights_ref[:, cut] * potential_factor(density), jnp.float32(0.0))
        scaled_ref[:, cut] = (factor * values).astype(jnp.bfloat16)

    @pl.loop(0, width // SLAB)
    def _(step):
        spot = pl.ds(pl.multiple_of(step * SLAB, SLAB), SLAB)
        block_ref[spot, :] = lax.dot_general(
            turned_ref[spot, :], scaled_ref[...], (((1,), (1,)), ((), ())), preferred_element_type=jnp.float32
        ).astype(jnp.bfloat16)

    def piece(target):
        there_row, there_col = target
        first = there_row * TILE + lax.rem(there_col, 2) * PART
        return block_ref.at[
            pl.ds(pl.multiple_of(first, PART), PART),
            pl.ds(pl.multiple_of(there_col // 2 * TILE, TILE), TILE),
        ]

    @pl.loop(1, DEVICES)
    def _(count):
        target = offset_device(row, col, lax.rem(count * STRIDE, DEVICES))
        pltpu.make_async_remote_copy(
            src_ref=piece(target),
            dst_ref=landed_ref.at[me],
            send_sem=all_send.at[1],
            recv_sem=all_recv.at[1],
            device_id=target,
            device_id_type=MESH,
        ).start()

    pltpu.make_async_copy(piece((row, col)), landed_ref.at[me], all_recv.at[1]).start()
    sums_ref[DEVICES] = jnp.zeros((PART, TILE), jnp.float32)
    rest = stage_ref.at[pl.ds(0, DEVICES - 1)]
    pltpu.make_async_copy(rest, rest, all_send.at[0]).wait()
    load_core.wait()
    load_chain.wait()
    save_rho = pltpu.make_async_copy(rho_ref, rho_hbm, load_sem.at[0])
    save_rho.start()
    pltpu.make_async_copy(landed_ref, landed_ref, all_recv.at[1]).wait()

    @pl.loop(0, DEVICES)
    def _(batch):
        sums_ref[batch] = sums_ref[chain_ref[0, batch]] + landed_ref[batch].astype(jnp.float32)

    def total(tile_row, half, tile):
        return sums_ref[chain_ref[1, tile_row * BS + half * (BS // 2) + tile]]

    for tile_row in range(BS):
        for tile in range(BS // 2):
            cut = slice(tile * TILE, (tile + 1) * TILE)
            give_ref[tile_row, :, cut] = total(tile_row, other, tile).astype(give_ref.dtype)
    pair = pltpu.make_async_remote_copy(
        src_ref=give_ref,
        dst_ref=got_ref,
        send_sem=back_send,
        recv_sem=back_recv,
        device_id=partner,
        device_id_type=MESH,
    )
    pair.start()

    def finish(first, value):
        spot = pl.ds(pl.multiple_of(first, PART), PART)
        xc_ref[spot, :] = value
        down = lax.broadcasted_iota(jnp.int32, value.shape, 0) + (row * BS * TILE + first)
        across = lax.broadcasted_iota(jnp.int32, value.shape, 1) + col * xc_ref.shape[1]
        shift = jnp.where(down == across, shift_ref[0], jnp.float32(0.0))
        start = shift + scale_ref[0] * (core_ref[spot, :] + value)
        start_ref[spot, :] = start
        rounded_ref[spot, :] = start.astype(jnp.bfloat16)

    for tile_row in range(BS):
        mine = jnp.concatenate([total(tile_row, side, tile) for tile in range(BS // 2)], axis=1)
        finish(tile_row * TILE + side * PART, mine)
    pair.wait()
    for tile_row in range(BS):
        finish(tile_row * TILE + other * PART, got_ref[tile_row].astype(jnp.float32))

    save_xc = pltpu.make_async_copy(xc_ref, xc_hbm, load_sem.at[1])
    save_xc.start()

    square(
        row, col, rounded_ref, start_ref, flag_ref, out_ref, rows_ref, cols_ref,
        row_send, row_recv, col_send, col_recv, core_send, core_recv, own_sem,
    )
    rest = landed_ref.at[pl.ds(0, DEVICES - 1)]
    pltpu.make_async_copy(rest, rest, all_send.at[1]).wait()
    save_out = pltpu.make_async_copy(out_ref, out_hbm, load_sem.at[2])
    save_out.start()
    save_rho.wait()
    save_xc.wait()
    save_out.wait()


def whole(shift, scale, flag, count, weights, tiles, density, basis, core_matrix):
    dma = pltpu.SemaphoreType.DMA
    tall, wide = core_matrix.shape
    points, width = basis.shape
    vmem = pl.BlockSpec(memory_space=pltpu.VMEM)
    smem = pl.BlockSpec(memory_space=pltpu.SMEM)
    hbm = pl.BlockSpec(memory_space=pl.ANY)
    bf16, f32 = jnp.bfloat16, jnp.float32
    return pl.pallas_call(
        whole_kernel,
        name="whole_kernel",
        out_shape=(
            jax.ShapeDtypeStruct((1, points), f32),
            jax.ShapeDtypeStruct((tall, wide), f32),
            jax.ShapeDtypeStruct((tall, wide), f32),
        ),
        in_specs=[smem, smem, smem, smem, vmem, hbm, hbm, hbm, hbm],
        out_specs=(hbm, hbm, hbm),
        scratch_shapes=[
            pltpu.SMEM((BLK, DEVICES), jnp.int32),
            pltpu.VMEM((BLK, DEVICES), jnp.int32),
            pltpu.VMEM((BLK, DEVICES), jnp.int32),
            pltpu.SMEM((BLK, DEVICES), jnp.int32),
            pltpu.VMEM((1, points), f32),
            pltpu.VMEM((tall, wide), f32),
            pltpu.VMEM((tall, wide), f32),
            pltpu.VMEM((points, width), bf16),
            pltpu.VMEM((tall, wide), f32),
            pltpu.VMEM((width, points), bf16),
            pltpu.VMEM((width, points), bf16),
            pltpu.VMEM((BS * BS, PART, TILE), bf16),
            pltpu.VMEM((DEVICES, PART, TILE), bf16),
            pltpu.VMEM((width, width), bf16),
            pltpu.VMEM((width, width), bf16),
            pltpu.VMEM((DEVICES, PART, TILE), bf16),
            pltpu.VMEM((DEVICES + 1, PART, TILE), f32),
            pltpu.VMEM((BS, PART, wide), bf16),
            pltpu.VMEM((BS, PART, wide), bf16),
            pltpu.VMEM((tall, wide), f32),
            pltpu.VMEM((tall, wide), bf16),
            pltpu.VMEM((2, RING, RING, tall // 2, wide), bf16),
            pltpu.VMEM((RING, 2, tall, wide), bf16),
            dma((5,)),
            dma((BS // 2,)),
            dma((BS // 2,)),
            dma((BS // 2,)),
            dma,
            dma,
            dma((2,)),
            dma((2,)),
            dma((2, RING, RING, 2)),
            dma((2, RING, RING, 2)),
            dma((RING, 2)),
            dma((RING, 2)),
            dma((RING,)),
            dma((RING,)),
            dma,
        ],
        compiler_params=pltpu.CompilerParams(
            collective_id=1, has_side_effects=True, vmem_limit_bytes=56 * 2**20
        ),
        cost_estimate=pl.CostEstimate(
            flops=4 * points * width * width + 2 * tall * wide * tall * 8, bytes_accessed=16 * 2**20, transcendentals=0
        ),
    )(shift, scale, flag, count, weights, tiles, density.reshape(BS, TILE, wide), basis, core_matrix)


def keep_kernel(*refs):
    count = (len(refs) - 1) // 3
    sems = refs[-1]
    loads, saves = [], []
    for i in range(count):
        source, target, held = refs[i], refs[count + i], refs[2 * count + i]
        loads.append(pltpu.make_async_copy(source, held, sems.at[0, i]))
        saves.append(pltpu.make_async_copy(held, target, sems.at[1, i]))
    for load in loads:
        load.start()
    for load, save in zip(loads, saves):
        load.wait()
        save.start()
    for save in saves:
        save.wait()


def kept(*arrays):
    hbm = pl.BlockSpec(memory_space=pl.ANY)
    return pl.pallas_call(
        keep_kernel,
        name="keep_kernel",
        out_shape=tuple(jax.ShapeDtypeStruct(a.shape, a.dtype) for a in arrays),
        in_specs=[hbm] * len(arrays),
        out_specs=(hbm,) * len(arrays),
        scratch_shapes=[pltpu.VMEM(a.shape, a.dtype) for a in arrays] + [pltpu.SemaphoreType.DMA((2, len(arrays)))],
    )(*arrays)


def body(
    basis_values,
    quad_weights,
    point_counts,
    basis_tiles,
    density,
    core_matrix,
    map_shift,
    map_scale,
    branch_flags,
):
    return kept(
        *whole(
            map_shift,
            map_scale,
            branch_flags,
            point_counts,
            quad_weights,
            basis_tiles.T,
            density,
            basis_values[0],
            core_matrix,
        )
    )


def solution(mesh):
    placed = (
        P(("row", "col"), None, None),
        P(("row", "col"), None),
        P(("row", "col")),
        P(),
        P("row", "col"),
        P("row", "col"),
        P(),
        P(),
        P(),
    )
    return jax.shard_map(
        body,
        mesh=mesh,
        in_specs=placed,
        out_specs=(P(("row", "col"), None), P("row", "col"), P("row", "col")),
        check_vma=False,
    )
```

```python
import jax
import jax.numpy as jnp
from jax import lax
from jax.experimental import pallas as pl
from jax.experimental.pallas import tpu as pltpu
from jax.sharding import PartitionSpec as P

MESH = pl.DeviceIdType.MESH
TILE = 128
PART = TILE // 2
BLK = 8
BS = 6
RING = 4
COLS = 16
DEVICES = 128
STRIDE = 37
SLATER = (3.0 / 3.141592653589793) ** (1.0 / 3.0)

def potential_factor(values):
    return -SLATER * (values * values + 1.0) ** (1.0 / 6.0)


def turn(value, step):
    return lax.rem(value + (step % RING), RING)


def offset_device(row, col, step):
    z, core = row // 2, lax.rem(row, 2)
    x, y = col // RING, lax.rem(col, RING)
    dx, dy = step // 32, lax.rem(step // 8, RING)
    dz, dcore = lax.rem(step // 2, RING), lax.rem(step, 2)
    there = lax.rem(z + dz, RING) * 2 + lax.rem(core + dcore, 2)
    return there, lax.rem(x + dx, RING) * RING + lax.rem(y + dy, RING)


CHUNK = 256
SLAB = 512


def greet_all(me):
    barrier = pltpu.get_barrier_semaphore()

    @pl.loop(1, DEVICES, unroll=8)
    def _(step):
        there = lax.rem(me + step, DEVICES)
        pl.semaphore_signal(
            barrier, inc=1, device_id=(there // COLS, lax.rem(there, COLS)), device_id_type=MESH
        )

    return barrier


def hop(place):
    position, part = place
    if position == 3:
        return 1, 0
    if position == 1:
        return -1, 0
    return (1, 3) if part == 0 else (-1, 1)


def whole_kernel(
    shift_ref,
    scale_ref,
    flag_ref,
    count_ref,
    weights_ref,
    tiles_hbm,
    dens_ref,
    basis_hbm,
    core_hbm,
    rho_hbm,
    xc_hbm,
    out_hbm,
    tiles_ref,
    tiles_vec,
    chain_vec,
    chain_ref,
    rho_ref,
    xc_ref,
    out_ref,
    basis_ref,
    core_ref,
    turned_ref,
    scaled_ref,
    both_ref,
    stage_ref,
    sub_ref,
    block_ref,
    landed_ref,
    sums_ref,
    band_ref,
    own_ref,
    depth_ref,
    give_ref,
    got_ref,
    piece_ref,
    cols_ref,
    total_ref,
    give_total_ref,
    got_total_ref,
    load_sem,
    in_send,
    in_recv,
    in_own,
    swap_send,
    swap_recv,
    total_send,
    total_recv,
    all_send,
    all_recv,
    row_send,
    row_recv,
    col_send,
    col_recv,
    core_send,
    core_recv,
    own_sem,
):
    row, col = lax.axis_index("row"), lax.axis_index("col")
    slot, side = col // 2, lax.rem(col, 2)
    other = 1 - side
    me = row * COLS + col
    partner = (row, slot * 2 + other)
    load_basis = pltpu.make_async_copy(basis_hbm, basis_ref, load_sem.at[0])
    load_core = pltpu.make_async_copy(core_hbm, core_ref, load_sem.at[1])
    half_wide = core_hbm.shape[2]
    near_cols = pl.ds(pl.multiple_of(side * half_wide, half_wide), half_wide)
    far_cols = pl.ds(pl.multiple_of(other * half_wide, half_wide), half_wide)
    near_part = pl.ds(pl.multiple_of(side * PART, PART), PART)
    far_part = pl.ds(pl.multiple_of(other * PART, PART), PART)
    mine_core = pltpu.make_async_copy(core_hbm.at[:, near_part], band_ref.at[:, :, near_cols], load_sem.at[5])
    swap_core = pltpu.make_async_remote_copy(
        src_ref=core_hbm.at[:, far_part],
        dst_ref=band_ref.at[:, :, near_cols],
        send_sem=swap_send.at[0],
        recv_sem=swap_recv.at[0],
        device_id=partner,
        device_id_type=MESH,
    )
    load_tiles = [
        pltpu.make_async_copy(tiles_hbm, tiles_ref, load_sem.at[2]),
        pltpu.make_async_copy(tiles_hbm, tiles_vec, load_sem.at[3]),
    ]
    for copy in load_tiles:
        copy.start()
    barrier = greet_all(me)
    for copy in load_tiles:
        copy.wait()

    pairs, mines = [], []
    for tile in range(BS // 2):
        cut = pl.ds(tile * TILE, TILE)
        spot = both_ref.at[pl.ds((side * (BS // 2) + tile) * BS, BS)]
        pairs.append(
            pltpu.make_async_remote_copy(
                src_ref=dens_ref.at[:, pl.ds(pl.multiple_of(other * PART, PART), PART), cut],
                dst_ref=spot,
                send_sem=in_send.at[tile],
                recv_sem=in_recv.at[tile],
                device_id=partner,
                device_id_type=MESH,
            )
        )
        mines.append(
            pltpu.make_async_copy(
                dens_ref.at[:, pl.ds(pl.multiple_of(side * PART, PART), PART), cut], spot, in_own.at[tile]
            )
        )
    for copy in mines:
        copy.start()
    pl.semaphore_wait(barrier, DEVICES - 1)
    for copy in pairs:
        copy.start()
    load_basis.start()
    load_core.start()
    mine_core.start()
    for copy in mines + pairs:
        copy.wait()

    spot_rows = pl.ds(pl.multiple_of(row * TILE + side * PART, PART), PART)
    spot_cols = pl.ds(pl.multiple_of(slot * TILE, TILE), TILE)

    def stage(target):
        batch = target[0] * COLS + target[1]
        tile_row = tiles_ref[row, batch] - row * BS
        tile_col = tiles_ref[slot, batch] - slot * BS
        stage_ref[batch] = both_ref[jnp.clip(tile_col * BS + tile_row, 0, BS * BS - 1)]
        return batch

    @pl.loop(1, DEVICES)
    def _(count):
        target = offset_device(row, col, lax.rem(count * STRIDE, DEVICES))
        batch = stage(target)
        pltpu.make_async_remote_copy(
            src_ref=stage_ref.at[batch],
            dst_ref=sub_ref.at[spot_rows, spot_cols],
            send_sem=all_send.at[0],
            recv_sem=all_recv.at[0],
            device_id=target,
            device_id_type=MESH,
        ).start()

    stage((row, col))
    pltpu.make_async_copy(stage_ref.at[me], sub_ref.at[spot_rows, spot_cols], all_recv.at[0]).start()

    key = (tiles_vec[pl.ds(row, 1), :] - row * BS) * BS + tiles_vec[pl.ds(slot, 1), :] - slot * BS
    across = jnp.broadcast_to(key, (DEVICES, DEVICES))
    down = across.T
    batch_down = lax.broadcasted_iota(jnp.int32, across.shape, 0)
    batch_across = lax.broadcasted_iota(jnp.int32, across.shape, 1)
    earlier = (down == across) & (batch_down < batch_across)
    prev = jnp.max(jnp.where(earlier, batch_down, -1), axis=0, keepdims=True)
    last = jnp.max(jnp.where(down == batch_across, batch_down, -1), axis=0, keepdims=True)
    chain_vec[...] = jnp.zeros_like(chain_vec)
    chain_vec[0:1, :] = jnp.where(prev < 0, DEVICES, prev)
    chain_vec[1:2, :] = jnp.where(last < 0, DEVICES, last)
    load_chain = pltpu.make_async_copy(chain_vec, chain_ref, load_sem.at[4])
    load_chain.start()

    points, width = basis_ref.shape
    load_basis.wait()

    @pl.loop(0, points // CHUNK)
    def _(step):
        first = pl.multiple_of(step * CHUNK, CHUNK)
        turned_ref[:, pl.ds(first, CHUNK)] = basis_ref[pl.ds(first, CHUNK), :].T

    pltpu.make_async_copy(sub_ref, sub_ref, all_recv.at[0]).wait()
    swap_core.start()

    @pl.loop(0, points // CHUNK)
    def _(step):
        cut = pl.ds(pl.multiple_of(step * CHUNK, CHUNK), CHUNK)
        mixed = jnp.dot(sub_ref[...], turned_ref[:, cut], preferred_element_type=jnp.float32)
        values = turned_ref[:, cut].astype(jnp.float32)
        density = jnp.sum(mixed * values, axis=0, keepdims=True)
        live = lax.broadcasted_iota(jnp.int32, density.shape, 1) + step * CHUNK < count_ref[0]
        density = jnp.where(live, density, jnp.float32(0.0))
        rho_ref[:, cut] = density
        factor = jnp.where(live, weights_ref[:, cut] * potential_factor(density), jnp.float32(0.0))
        scaled_ref[:, cut] = (factor * values).astype(jnp.bfloat16)

    @pl.loop(0, width // SLAB)
    def _(step):
        spot = pl.ds(pl.multiple_of(step * SLAB, SLAB), SLAB)
        block_ref[spot, :] = lax.dot_general(
            turned_ref[spot, :], scaled_ref[...], (((1,), (1,)), ((), ())), preferred_element_type=jnp.float32
        ).astype(jnp.bfloat16)

    def piece(target):
        there_row, there_col = target
        first = there_row * TILE + lax.rem(there_col, 2) * PART
        return block_ref.at[
            pl.ds(pl.multiple_of(first, PART), PART),
            pl.ds(pl.multiple_of(there_col // 2 * TILE, TILE), TILE),
        ]

    @pl.loop(1, DEVICES)
    def _(count):
        target = offset_device(row, col, lax.rem(count * STRIDE, DEVICES))
        pltpu.make_async_remote_copy(
            src_ref=piece(target),
            dst_ref=landed_ref.at[me],
            send_sem=all_send.at[1],
            recv_sem=all_recv.at[1],
            device_id=target,
            device_id_type=MESH,
        ).start()

    pltpu.make_async_copy(piece((row, col)), landed_ref.at[me], all_recv.at[1]).start()
    sums_ref[DEVICES] = jnp.zeros((PART, TILE), jnp.float32)
    rest = stage_ref.at[pl.ds(0, DEVICES - 1)]
    pltpu.make_async_copy(rest, rest, all_send.at[0]).wait()
    load_core.wait()
    load_chain.wait()
    save_rho = pltpu.make_async_copy(rho_ref, rho_hbm, load_sem.at[0])
    save_rho.start()
    pltpu.make_async_copy(landed_ref, landed_ref, all_recv.at[1]).wait()

    @pl.loop(0, DEVICES)
    def _(batch):
        sums_ref[batch] = sums_ref[chain_ref[0, batch]] + landed_ref[batch].astype(jnp.float32)

    def total(tile_row, tile):
        return sums_ref[chain_ref[1, tile_row * BS + tile]]

    mine_core.wait()
    swap_core.wait()
    wide = BS * TILE
    for tile_row in range(BS):
        value = jnp.concatenate([total(tile_row, tile) for tile in range(BS)], axis=1)
        down = lax.broadcasted_iota(jnp.int32, value.shape, 0) + (row * wide + tile_row * TILE + side * PART)
        across = lax.broadcasted_iota(jnp.int32, value.shape, 1) + slot * wide
        shift = jnp.where(down == across, shift_ref[0], jnp.float32(0.0))
        start = shift + scale_ref[0] * (band_ref[tile_row] + value)
        band_ref[tile_row] = start
        spot = slice(tile_row * PART, (tile_row + 1) * PART)
        own_ref[spot, :] = start.astype(jnp.bfloat16)
        for depth in (0, 1):
            lanes = [start[:, tile * TILE + depth * PART : tile * TILE + (depth + 1) * PART] for tile in range(BS)]
            depth_ref[depth, spot, :] = jnp.concatenate(lanes, axis=1).astype(jnp.bfloat16)

    z, core = row // 2, lax.rem(row, 2)
    x, y = col // RING, lax.rem(col, RING)
    piece_rows = own_ref.shape[0]

    def device(axis, step):
        if axis == "x":
            return (row, turn(x, step) * RING + y)
        if axis == "y":
            return (row, x * RING + turn(y, step))
        if axis == "z":
            return (turn(z, step) * 2 + core, col)
        return (z * 2 + 1 - core, col)

    def piece_at(dx, dy):
        if dx == 0 and dy == 0:
            return depth_ref.at[side]
        return piece_ref.at[dx, dy]

    def y_copy(dy):
        step = -dy
        return pltpu.make_async_remote_copy(
            src_ref=depth_ref.at[side if dy == 2 else other],
            dst_ref=piece_ref.at[0, dy],
            send_sem=row_send.at[0, dy, 0],
            recv_sem=row_recv.at[0, dy, 0],
            device_id=device("y", step),
            device_id_type=MESH,
        )

    def x_copy(dx, dy, part=0):
        step, source = hop((dx, part))
        src, dst = piece_at(source, dy), piece_ref.at[dx, dy]
        if dx == 2:
            part_rows = pl.ds(part * (piece_rows // 2), piece_rows // 2)
            src, dst = src.at[part_rows], dst.at[part_rows]
        return pltpu.make_async_remote_copy(
            src_ref=src,
            dst_ref=dst,
            send_sem=row_send.at[dx, dy, part],
            recv_sem=row_recv.at[dx, dy, part],
            device_id=device("x", step),
            device_id_type=MESH,
        )

    def z_copy(dz, part=0):
        step, source = hop((dz, part))
        place = turn(z, source)
        src = own_ref if source == 0 else cols_ref.at[place, core]
        dst = cols_ref.at[place, core]
        if dz == 2:
            part_rows = pl.ds(part * (piece_rows // 2), piece_rows // 2)
            src, dst = src.at[part_rows], dst.at[part_rows]
        return pltpu.make_async_remote_copy(
            src_ref=src,
            dst_ref=dst,
            send_sem=col_send.at[dz, part],
            recv_sem=col_recv.at[dz, part],
            device_id=device("z", step),
            device_id_type=MESH,
        )

    def core_copy(dz):
        place = turn(z, dz)
        return pltpu.make_async_remote_copy(
            src_ref=own_ref if dz == 0 else cols_ref.at[place, core],
            dst_ref=cols_ref.at[place, core],
            send_sem=core_send.at[dz],
            recv_sem=core_recv.at[dz],
            device_id=device("core", 1),
            device_id_type=MESH,
        )

    started = []

    def go(copy):
        copy.start()
        started.append(copy)

    for dx in (3, 1):
        go(x_copy(dx, 0))
    for dy in (2, 3, 1):
        go(y_copy(dy))
    for dz in (3, 1):
        go(z_copy(dz))
    go(core_copy(0))
    mine = pltpu.make_async_copy(own_ref, cols_ref.at[z, core], own_sem)
    mine.start()

    def strip(tile_row, half):
        found = [sums_ref[chain_ref[1, tile_row * BS + half * (BS // 2) + tile]] for tile in range(BS // 2)]
        return jnp.concatenate(found, axis=1)

    for tile_row in range(BS):
        give_ref[tile_row] = strip(tile_row, other)
    pair = pltpu.make_async_remote_copy(
        src_ref=give_ref,
        dst_ref=got_ref,
        send_sem=swap_send.at[1],
        recv_sem=swap_recv.at[1],
        device_id=partner,
        device_id_type=MESH,
    )
    go(pair)
    for tile_row in range(BS):
        xc_ref[pl.ds(pl.multiple_of(tile_row * TILE + side * PART, PART), PART), :] = strip(tile_row, side)

    def pass_on(dy):
        for dx, part in ((3, 0), (1, 1)):
            x_copy(dx, dy).wait_recv()
            go(x_copy(2, dy, part))

    pass_on(0)
    for dy in (2, 3, 1):
        y_copy(dy).wait_recv()
        for dx in (3, 1):
            go(x_copy(dx, dy))
    for dz, part in ((3, 0), (1, 1)):
        z_copy(dz).wait_recv()
        go(z_copy(2, part))
        go(core_copy(dz))
    pass_on(2)
    for part in (0, 1):
        z_copy(2, part).wait_recv()
    go(core_copy(2))

    def multiply(dx, dy):
        there_x, there_y = turn(x, dx), turn(y, dy)
        factor = cols_ref[there_x, there_y // 2]
        product = jnp.dot(piece_at(dx, dy)[...], factor, preferred_element_type=jnp.float32)
        group = dy % 2
        if dx == 0 and dy in (0, 3):
            total_ref[group] = product
        else:
            total_ref[group] += product

    def swap_total(group):
        kind = side if group == 0 else other
        give_total_ref[group] = total_ref[group, :, far_cols].astype(jnp.bfloat16)
        return pltpu.make_async_remote_copy(
            src_ref=give_total_ref.at[group],
            dst_ref=got_total_ref.at[kind],
            send_sem=total_send.at[group],
            recv_sem=total_recv.at[kind],
            device_id=partner,
            device_id_type=MESH,
        )

    mine.wait()
    for dz in range(RING):
        core_copy(dz).wait_recv()
    multiply(0, 0)
    for dx in (3, 1):
        multiply(dx, 0)
    for part in (0, 1):
        x_copy(2, 0, part).wait_recv()
    multiply(2, 0)
    for dx in (0, 3, 1):
        multiply(dx, 2)
    pass_on(3)
    for part in (0, 1):
        x_copy(2, 2, part).wait_recv()
    multiply(2, 2)
    go(swap_total(0))
    for dx in (0, 3, 1):
        multiply(dx, 3)
    multiply(0, 1)
    pair.wait_recv()
    for tile_row in range(BS):
        xc_ref[pl.ds(pl.multiple_of(tile_row * TILE + other * PART, PART), PART), :] = got_ref[tile_row]
    save_xc = pltpu.make_async_copy(xc_ref, xc_hbm, load_sem.at[1])
    save_xc.start()
    pass_on(1)
    for dx in (3, 1):
        multiply(dx, 1)
    for dy in (3, 1):
        for part in (0, 1):
            x_copy(2, dy, part).wait_recv()
        multiply(2, dy)
    go(swap_total(1))

    keep = flag_ref[0] == 0
    sign = jnp.where(keep, 1.0, -1.0)
    twice = jnp.where(keep, 0.0, 2.0)

    def finish(group):
        kind = side if group == 0 else other
        got = pltpu.make_async_copy(got_total_ref.at[kind], got_total_ref.at[kind], total_recv.at[kind])
        got.wait()
        for tile_row in range(BS):
            spot = slice(tile_row * PART, (tile_row + 1) * PART)
            first = pl.multiple_of(tile_row * TILE + kind * PART, PART)
            if group == 0:
                start = band_ref[tile_row, :, near_cols]
            else:
                down = lax.broadcasted_iota(jnp.int32, (PART, half_wide), 0) + (row * wide + first)
                across = lax.broadcasted_iota(jnp.int32, (PART, half_wide), 1) + col * half_wide
                shift = jnp.where(down == across, shift_ref[0], jnp.float32(0.0))
                start = shift + scale_ref[0] * (core_ref[tile_row, far_part] + xc_ref[pl.ds(first, PART), :])
            square = total_ref[group, spot, near_cols] + got_total_ref[kind, spot, :].astype(jnp.float32)
            out_ref[pl.ds(first, PART), :] = sign * square + twice * start

    finish(1)
    finish(0)
    save_out = pltpu.make_async_copy(out_ref, out_hbm, load_sem.at[2])
    save_out.start()
    for copy in started:
        copy.wait_send()
    rest = landed_ref.at[pl.ds(0, DEVICES - 1)]
    pltpu.make_async_copy(rest, rest, all_send.at[1]).wait()
    save_rho.wait()
    save_xc.wait()
    save_out.wait()


def whole(shift, scale, flag, count, weights, tiles, density, basis, core_matrix):
    dma = pltpu.SemaphoreType.DMA
    tall, wide = core_matrix.shape
    points, width = basis.shape
    vmem = pl.BlockSpec(memory_space=pltpu.VMEM)
    smem = pl.BlockSpec(memory_space=pltpu.SMEM)
    hbm = pl.BlockSpec(memory_space=pl.ANY)
    bf16, f32 = jnp.bfloat16, jnp.float32
    return pl.pallas_call(
        whole_kernel,
        name="whole_kernel",
        out_shape=(
            jax.ShapeDtypeStruct((1, points), f32),
            jax.ShapeDtypeStruct((tall, wide), f32),
            jax.ShapeDtypeStruct((tall, wide), f32),
        ),
        in_specs=[smem, smem, smem, smem, vmem, hbm, hbm, hbm, hbm],
        out_specs=(hbm, hbm, hbm),
        scratch_shapes=[
            pltpu.SMEM((BLK, DEVICES), jnp.int32),
            pltpu.VMEM((BLK, DEVICES), jnp.int32),
            pltpu.VMEM((BLK, DEVICES), jnp.int32),
            pltpu.SMEM((BLK, DEVICES), jnp.int32),
            pltpu.VMEM((1, points), f32),
            pltpu.VMEM((tall, wide), f32),
            pltpu.VMEM((tall, wide), f32),
            pltpu.VMEM((points, width), bf16),
            pltpu.VMEM((BS, TILE, wide), f32),
            pltpu.VMEM((width, points), bf16),
            pltpu.VMEM((width, points), bf16),
            pltpu.VMEM((BS * BS, PART, TILE), bf16),
            pltpu.VMEM((DEVICES, PART, TILE), bf16),
            pltpu.VMEM((width, width), bf16),
            pltpu.VMEM((width, width), bf16),
            pltpu.VMEM((DEVICES, PART, TILE), bf16),
            pltpu.VMEM((DEVICES + 1, PART, TILE), f32),
            pltpu.VMEM((BS, PART, 2 * wide), f32),
            pltpu.VMEM((BS * PART, 2 * wide), bf16),
            pltpu.VMEM((2, BS * PART, wide), bf16),
            pltpu.VMEM((BS, PART, wide), f32),
            pltpu.VMEM((BS, PART, wide), f32),
            pltpu.VMEM((RING, RING, BS * PART, wide), bf16),
            pltpu.VMEM((RING, 2, BS * PART, 2 * wide), bf16),
            pltpu.VMEM((2, BS * PART, 2 * wide), f32),
            pltpu.VMEM((2, BS * PART, wide), bf16),
            pltpu.VMEM((2, BS * PART, wide), bf16),
            dma((6,)),
            dma((BS // 2,)),
            dma((BS // 2,)),
            dma((BS // 2,)),
            dma((2,)),
            dma((2,)),
            dma((2,)),
            dma((2,)),
            dma((2,)),
            dma((2,)),
            dma((RING, RING, 2)),
            dma((RING, RING, 2)),
            dma((RING, 2)),
            dma((RING, 2)),
            dma((RING,)),
            dma((RING,)),
            dma,
        ],
        compiler_params=pltpu.CompilerParams(
            collective_id=1, has_side_effects=True, vmem_limit_bytes=56 * 2**20
        ),
        cost_estimate=pl.CostEstimate(
            flops=4 * points * width * width + 2 * tall * wide * tall * 8, bytes_accessed=16 * 2**20, transcendentals=0
        ),
    )(shift, scale, flag, count, weights, tiles, density.reshape(BS, TILE, wide), basis, core_matrix.reshape(BS, TILE, wide))


def keep_kernel(*refs):
    count = (len(refs) - 1) // 3
    sems = refs[-1]
    loads, saves = [], []
    for i in range(count):
        source, target, held = refs[i], refs[count + i], refs[2 * count + i]
        loads.append(pltpu.make_async_copy(source, held, sems.at[0, i]))
        saves.append(pltpu.make_async_copy(held, target, sems.at[1, i]))
    for load in loads:
        load.start()
    for load, save in zip(loads, saves):
        load.wait()
        save.start()
    for save in saves:
        save.wait()


def kept(*arrays):
    hbm = pl.BlockSpec(memory_space=pl.ANY)
    return pl.pallas_call(
        keep_kernel,
        name="keep_kernel",
        out_shape=tuple(jax.ShapeDtypeStruct(a.shape, a.dtype) for a in arrays),
        in_specs=[hbm] * len(arrays),
        out_specs=(hbm,) * len(arrays),
        scratch_shapes=[pltpu.VMEM(a.shape, a.dtype) for a in arrays] + [pltpu.SemaphoreType.DMA((2, len(arrays)))],
    )(*arrays)


def body(
    basis_values,
    quad_weights,
    point_counts,
    basis_tiles,
    density,
    core_matrix,
    map_shift,
    map_scale,
    branch_flags,
):
    return kept(
        *whole(
            map_shift,
            map_scale,
            branch_flags,
            point_counts,
            quad_weights,
            basis_tiles.T,
            density,
            basis_values[0],
            core_matrix,
        )
    )


def solution(mesh):
    placed = (
        P(("row", "col"), None, None),
        P(("row", "col"), None),
        P(("row", "col")),
        P(),
        P("row", "col"),
        P("row", "col"),
        P(),
        P(),
        P(),
    )
    return jax.shard_map(
        body,
        mesh=mesh,
        in_specs=placed,
        out_specs=(P(("row", "col"), None), P("row", "col"), P("row", "col")),
        check_vma=False,
    )
```

```python
import jax
import jax.numpy as jnp
from jax import lax
from jax.experimental import pallas as pl
from jax.experimental.pallas import tpu as pltpu
from jax.sharding import PartitionSpec as P

MESH = pl.DeviceIdType.MESH
TILE = 128
PART = TILE // 2
BLK = 8
BS = 6
RING = 4
COLS = 16
DEVICES = 128
STRIDE = 37
SLATER = (3.0 / 3.141592653589793) ** (1.0 / 3.0)

def potential_factor(values):
    return -SLATER * (values * values + 1.0) ** (1.0 / 6.0)


def turn(value, step):
    return lax.rem(value + (step % RING), RING)


def offset_device(row, col, half, count):
    step = lax.rem(count * STRIDE, DEVICES // 2)
    z, core = row // 2, lax.rem(row, 2)
    x, y = col // RING, lax.rem(col, RING)
    dx, dy = step // 16, lax.rem(step // 4, RING)
    dz, dcore = half + lax.rem(step // 2, 2) * 2, lax.rem(step, 2)
    there = lax.rem(z + dz, RING) * 2 + lax.rem(core + dcore, 2)
    return there, lax.rem(x + dx, RING) * RING + lax.rem(y + dy, RING)


CHUNK = 256
STEPS = 32767.0
JOBS = ((0, 0, 192), (0, 192, 192), (3, 0, 384), (1, 0, 384), (2, 0, 256), (2, 256, 128))


def greet_all(me):
    barrier = pltpu.get_barrier_semaphore()

    @pl.loop(1, DEVICES, unroll=8)
    def _(step):
        there = lax.rem(me + step, DEVICES)
        pl.semaphore_signal(
            barrier, inc=1, device_id=(there // COLS, lax.rem(there, COLS)), device_id_type=MESH
        )

    return barrier


def hop(place):
    position, part = place
    if position == 3:
        return 1, 0
    if position == 1:
        return -1, 0
    return (1, 3) if part == 0 else (-1, 1)


def whole_kernel(
    shift_ref,
    scale_ref,
    flag_ref,
    count_ref,
    weights_ref,
    tiles_hbm,
    dens_ref,
    basis_hbm,
    core_hbm,
    rho_hbm,
    xc_hbm,
    out_hbm,
    tiles_ref,
    tiles_vec,
    chain_vec,
    chain_ref,
    rho_ref,
    xc_ref,
    out_ref,
    basis_ref,
    core_ref,
    turned_ref,
    scaled_ref,
    both_ref,
    stage_ref,
    sub_ref,
    block_ref,
    landed_ref,
    sums_ref,
    band_ref,
    own_ref,
    depth_ref,
    give_core_ref,
    got_core_ref,
    give_most_ref,
    got_most_ref,
    give_ref,
    got_ref,
    piece_ref,
    cols_ref,
    total_ref,
    give_total_ref,
    got_total_ref,
    load_sem,
    in_send,
    in_recv,
    in_own,
    swap_send,
    swap_recv,
    total_send,
    total_recv,
    all_send,
    all_recv,
    in_halves,
    row_send,
    row_recv,
    y_send,
    y_recv,
    save_sem,
    col_send,
    col_recv,
    core_send,
    core_recv,
    own_sem,
):
    row, col = lax.axis_index("row"), lax.axis_index("col")
    slot, side = col // 2, lax.rem(col, 2)
    other = 1 - side
    me = row * COLS + col
    partner = (row, slot * 2 + other)
    load_basis = pltpu.make_async_copy(basis_hbm, basis_ref, load_sem.at[0])
    load_core = pltpu.make_async_copy(core_hbm, core_ref, load_sem.at[1])
    half_wide = core_hbm.shape[2]
    near_cols = pl.ds(pl.multiple_of(side * half_wide, half_wide), half_wide)
    far_cols = pl.ds(pl.multiple_of(other * half_wide, half_wide), half_wide)
    near_part = pl.ds(pl.multiple_of(side * PART, PART), PART)
    far_part = pl.ds(pl.multiple_of(other * PART, PART), PART)
    mine_core = pltpu.make_async_copy(core_hbm.at[:, near_part], band_ref.at[:, :, near_cols], load_sem.at[5])
    swap_core = pltpu.make_async_remote_copy(
        src_ref=give_core_ref,
        dst_ref=got_core_ref,
        send_sem=swap_send.at[0],
        recv_sem=swap_recv.at[0],
        device_id=partner,
        device_id_type=MESH,
    )
    swap_most = pltpu.make_async_remote_copy(
        src_ref=give_most_ref,
        dst_ref=got_most_ref,
        send_sem=swap_send.at[2],
        recv_sem=swap_recv.at[2],
        device_id=partner,
        device_id_type=MESH,
    )
    load_tiles = [
        pltpu.make_async_copy(tiles_hbm, tiles_ref, load_sem.at[2]),
        pltpu.make_async_copy(tiles_hbm, tiles_vec, load_sem.at[3]),
    ]
    for copy in load_tiles:
        copy.start()
    barrier = greet_all(me)
    for copy in load_tiles:
        copy.wait()

    pairs, mines = [], []
    for tile in range(BS // 2):
        cut = pl.ds(tile * TILE, TILE)
        spot = both_ref.at[pl.ds((side * (BS // 2) + tile) * BS, BS)]
        pairs.append(
            pltpu.make_async_remote_copy(
                src_ref=dens_ref.at[:, pl.ds(pl.multiple_of(other * PART, PART), PART), cut],
                dst_ref=spot,
                send_sem=in_send.at[tile],
                recv_sem=in_recv.at[tile],
                device_id=partner,
                device_id_type=MESH,
            )
        )
        mines.append(
            pltpu.make_async_copy(
                dens_ref.at[:, pl.ds(pl.multiple_of(side * PART, PART), PART), cut], spot, in_own.at[tile]
            )
        )
    for copy in mines:
        copy.start()
    pl.semaphore_wait(barrier, DEVICES - 1)
    for copy in pairs:
        copy.start()
    load_core.start()
    load_basis.start()
    mine_core.start()
    for copy in mines + pairs:
        copy.wait()

    depth_z, depth_core = row // 2, lax.rem(row, 2)
    spot_cols = pl.ds(pl.multiple_of(slot * TILE, TILE), TILE)

    def landing(half):
        first = (depth_z // 2) * 2 * TILE + depth_core * TILE + side * PART
        return sub_ref.at[half, pl.ds(pl.multiple_of(first, PART), PART), spot_cols]

    def stage(target):
        batch = target[0] * COLS + target[1]
        tile_row = tiles_ref[row, batch] - row * BS
        tile_col = tiles_ref[slot, batch] - slot * BS
        stage_ref[batch] = both_ref[jnp.clip(tile_col * BS + tile_row, 0, BS * BS - 1)]
        return batch

    for half in (0, 1):

        @pl.loop(1 - half, DEVICES // 2)
        def _(count, half=half):
            target = offset_device(row, col, half, count)
            batch = stage(target)
            pltpu.make_async_remote_copy(
                src_ref=stage_ref.at[batch],
                dst_ref=landing(half),
                send_sem=all_send.at[0],
                recv_sem=in_halves.at[half],
                device_id=target,
                device_id_type=MESH,
            ).start()

        if half == 0:
            stage((row, col))
            pltpu.make_async_copy(stage_ref.at[me], landing(0), in_halves.at[0]).start()

    key = (tiles_vec[pl.ds(row, 1), :] - row * BS) * BS + tiles_vec[pl.ds(slot, 1), :] - slot * BS
    across = jnp.broadcast_to(key, (DEVICES, DEVICES))
    down = across.T
    batch_down = lax.broadcasted_iota(jnp.int32, across.shape, 0)
    batch_across = lax.broadcasted_iota(jnp.int32, across.shape, 1)
    earlier = (down == across) & (batch_down < batch_across)
    prev = jnp.max(jnp.where(earlier, batch_down, -1), axis=0, keepdims=True)
    last = jnp.max(jnp.where(down == batch_across, batch_down, -1), axis=0, keepdims=True)
    chain_vec[...] = jnp.zeros_like(chain_vec)
    chain_vec[0:1, :] = jnp.where(prev < 0, DEVICES, prev)
    chain_vec[1:2, :] = jnp.where(last < 0, DEVICES, last)
    load_chain = pltpu.make_async_copy(chain_vec, chain_ref, load_sem.at[4])
    load_chain.start()

    load_core.wait()
    most = jnp.zeros((1, 1), jnp.float32)
    for tile_row in range(BS):
        strip_most = jnp.max(jnp.abs(core_ref[tile_row, far_part]), axis=0, keepdims=True)
        most = jnp.maximum(most, jnp.max(strip_most, axis=1, keepdims=True))
    most = jnp.maximum(most, 1e-30)
    give_most_ref[...] = jnp.broadcast_to(most, give_most_ref.shape)
    for tile_row in range(BS):
        steps = jnp.round(core_ref[tile_row, far_part] * (STEPS / most))
        give_core_ref[tile_row] = steps.astype(jnp.int32).astype(jnp.int16)

    points, width = basis_ref.shape
    load_basis.wait()

    @pl.loop(0, points // CHUNK)
    def _(step):
        first = pl.multiple_of(step * CHUNK, CHUNK)
        turned_ref[:, pl.ds(first, CHUNK)] = basis_ref[pl.ds(first, CHUNK), :].T

    def band(half, which):
        place = which * 2 + lax.rem(depth_z + half, 2)
        return pl.ds(pl.multiple_of(place * 2 * TILE, 2 * TILE), 2 * TILE)

    for half in (0, 1):
        landed_half = pltpu.make_async_copy(sub_ref.at[half], sub_ref.at[half], in_halves.at[half])
        landed_half.wait()
        if half == 1:
            swap_core.start()
            swap_most.start()

        @pl.loop(0, points // CHUNK)
        def _(step, half=half):
            cut = pl.ds(pl.multiple_of(step * CHUNK, CHUNK), CHUNK)
            mixed = jnp.dot(sub_ref[half], turned_ref[:, cut], preferred_element_type=jnp.float32)
            density = jnp.zeros((1, CHUNK), jnp.float32)
            for which in (0, 1):
                values = turned_ref[band(half, which), cut].astype(jnp.float32)
                part = mixed[which * 2 * TILE : (which + 1) * 2 * TILE]
                density += jnp.sum(part * values, axis=0, keepdims=True)
            if half == 0:
                rho_ref[:, cut] = density
                return
            density += rho_ref[:, cut]
            live = lax.broadcasted_iota(jnp.int32, density.shape, 1) + step * CHUNK < count_ref[0]
            density = jnp.where(live, density, jnp.float32(0.0))
            rho_ref[:, cut] = density
            factor = jnp.where(live, weights_ref[:, cut] * potential_factor(density), jnp.float32(0.0))
            scaled_ref[:, cut] = (factor * turned_ref[:, cut].astype(jnp.float32)).astype(jnp.bfloat16)

    def piece(target):
        there_row, there_col = target
        first = there_row * TILE + lax.rem(there_col, 2) * PART
        return block_ref.at[
            pl.ds(pl.multiple_of(first, PART), PART),
            pl.ds(pl.multiple_of(there_col // 2 * TILE, TILE), TILE),
        ]

    for half in (0, 1):
        bands = [band(half, 0), band(half, 1)]
        values = jnp.concatenate([turned_ref[spot, :] for spot in bands], axis=0)
        result = lax.dot_general(
            values, scaled_ref[...], (((1,), (1,)), ((), ())), preferred_element_type=jnp.float32
        ).astype(jnp.bfloat16)
        for which in (0, 1):
            block_ref[bands[which], :] = result[which * 2 * TILE : (which + 1) * 2 * TILE]

        @pl.loop(1 - half, DEVICES // 2)
        def _(count, half=half):
            target = offset_device(row, col, half, count)
            pltpu.make_async_remote_copy(
                src_ref=piece(target),
                dst_ref=landed_ref.at[me],
                send_sem=all_send.at[1],
                recv_sem=all_recv.at[1],
                device_id=target,
                device_id_type=MESH,
            ).start()

        if half == 0:
            pltpu.make_async_copy(piece((row, col)), landed_ref.at[me], all_recv.at[1]).start()

    sums_ref[DEVICES] = jnp.zeros((PART, TILE), jnp.float32)
    rest = stage_ref.at[pl.ds(0, DEVICES - 1)]
    pltpu.make_async_copy(rest, rest, all_send.at[0]).wait()
    load_chain.wait()
    save_rho = pltpu.make_async_copy(rho_ref, rho_hbm, load_sem.at[0])
    save_rho.start()
    pltpu.make_async_copy(landed_ref, landed_ref, all_recv.at[1]).wait()

    @pl.loop(0, DEVICES)
    def _(batch):
        sums_ref[batch] = sums_ref[chain_ref[0, batch]] + landed_ref[batch].astype(jnp.float32)

    def total(tile_row, tile):
        return sums_ref[chain_ref[1, tile_row * BS + tile]]

    mine_core.wait()
    swap_core.wait()
    swap_most.wait()
    most = got_most_ref[0:1, 0:1] / STEPS
    wide = BS * TILE
    for tile_row in range(BS):
        value = jnp.concatenate([total(tile_row, tile) for tile in range(BS)], axis=1)
        down = lax.broadcasted_iota(jnp.int32, value.shape, 0) + (row * wide + tile_row * TILE + side * PART)
        across = lax.broadcasted_iota(jnp.int32, value.shape, 1) + slot * wide
        shift = jnp.where(down == across, shift_ref[0], jnp.float32(0.0))
        band_ref[tile_row, :, far_cols] = got_core_ref[tile_row].astype(jnp.int32).astype(jnp.float32) * most
        start = shift + scale_ref[0] * (band_ref[tile_row] + value)
        band_ref[tile_row] = start
        spot = slice(tile_row * PART, (tile_row + 1) * PART)
        own_ref[spot, :] = start.astype(jnp.bfloat16)
        for depth in (0, 1):
            lanes = [start[:, tile * TILE + depth * PART : tile * TILE + (depth + 1) * PART] for tile in range(BS)]
            depth_ref[depth, spot, :] = jnp.concatenate(lanes, axis=1).astype(jnp.bfloat16)

    z, core = row // 2, lax.rem(row, 2)
    x, y = col // RING, lax.rem(col, RING)
    piece_rows = own_ref.shape[0]

    def device(axis, step):
        if axis == "x":
            return (row, turn(x, step) * RING + y)
        if axis == "y":
            return (row, x * RING + turn(y, step))
        if axis == "z":
            return (turn(z, step) * 2 + core, col)
        return (z * 2 + 1 - core, col)

    def piece_at(dx, dy):
        if dx == 0 and dy == 0:
            return depth_ref.at[side]
        return piece_ref.at[dx, dy]

    def y_copy(dy):
        step = -dy
        return pltpu.make_async_remote_copy(
            src_ref=depth_ref.at[side if dy == 2 else other],
            dst_ref=piece_ref.at[0, dy],
            send_sem=y_send.at[dy],
            recv_sem=y_recv.at[dy],
            device_id=device("y", step),
            device_id_type=MESH,
        )

    def x_copy(job, dx, part=0):
        dy, first, count = JOBS[job]
        step, source = hop((dx, part))
        if dx == 2:
            first, count = first + part * (count // 2), count // 2
        spot = pl.ds(first, count)
        return pltpu.make_async_remote_copy(
            src_ref=piece_at(source, dy).at[spot],
            dst_ref=piece_ref.at[dx, dy].at[spot],
            send_sem=row_send.at[job, dx, part],
            recv_sem=row_recv.at[job, dx, part],
            device_id=device("x", step),
            device_id_type=MESH,
        )

    def z_copy(dz, part=0):
        step, source = hop((dz, part))
        place = turn(z, source)
        src = own_ref if source == 0 else cols_ref.at[place, core]
        dst = cols_ref.at[place, core]
        if dz == 2:
            part_rows = pl.ds(part * (piece_rows // 2), piece_rows // 2)
            src, dst = src.at[part_rows], dst.at[part_rows]
        return pltpu.make_async_remote_copy(
            src_ref=src,
            dst_ref=dst,
            send_sem=col_send.at[dz, part],
            recv_sem=col_recv.at[dz, part],
            device_id=device("z", step),
            device_id_type=MESH,
        )

    def core_copy(dz):
        place = turn(z, dz)
        return pltpu.make_async_remote_copy(
            src_ref=own_ref if dz == 0 else cols_ref.at[place, core],
            dst_ref=cols_ref.at[place, core],
            send_sem=core_send.at[dz],
            recv_sem=core_recv.at[dz],
            device_id=device("core", 1),
            device_id_type=MESH,
        )

    started = []

    def go(copy):
        copy.start()
        started.append(copy)

    def start_job(job):
        for dx in (3, 1):
            go(x_copy(job, dx))

    def pass_on(job):
        for dx, part in ((3, 0), (1, 1)):
            x_copy(job, dx).wait_recv()
            go(x_copy(job, 2, part))

    def far_landed(job):
        for part in (0, 1):
            x_copy(job, 2, part).wait_recv()

    start_job(0)
    start_job(1)
    for dy in (3, 1, 2):
        go(y_copy(dy))
    for dz in (3, 1):
        go(z_copy(dz))
    go(core_copy(0))
    mine = pltpu.make_async_copy(own_ref, cols_ref.at[z, core], own_sem)
    mine.start()

    def strip(tile_row, half):
        found = [sums_ref[chain_ref[1, tile_row * BS + half * (BS // 2) + tile]] for tile in range(BS // 2)]
        return jnp.concatenate(found, axis=1)

    for tile_row in range(BS):
        give_ref[tile_row] = strip(tile_row, other)
    pair = pltpu.make_async_remote_copy(
        src_ref=give_ref,
        dst_ref=got_ref,
        send_sem=swap_send.at[1],
        recv_sem=swap_recv.at[1],
        device_id=partner,
        device_id_type=MESH,
    )
    for tile_row in range(BS):
        xc_ref[pl.ds(pl.multiple_of(tile_row * TILE + side * PART, PART), PART), :] = strip(tile_row, side)

    pass_on(0)
    y_copy(3).wait_recv()
    start_job(2)
    pass_on(1)
    y_copy(1).wait_recv()
    start_job(3)
    for dz, part in ((3, 0), (1, 1)):
        z_copy(dz).wait_recv()
        go(z_copy(2, part))
        go(core_copy(dz))
    y_copy(2).wait_recv()
    go(pair)
    pass_on(2)
    start_job(4)
    for part in (0, 1):
        z_copy(2, part).wait_recv()
    go(core_copy(2))

    def multiply(job, dx):
        dy, first, count = JOBS[job]
        spot = pl.ds(first, count)
        there_x, there_y = turn(x, dx), turn(y, dy)
        factor = cols_ref[there_x, there_y // 2]
        product = jnp.dot(piece_at(dx, dy)[spot, :], factor, preferred_element_type=jnp.float32)
        group = dy % 2
        if dx == 0 and dy in (0, 3):
            total_ref[group, spot, :] = product
        else:
            total_ref[group, spot, :] += product

    cuts = ((1, 0, 384), (0, 0, 256), (0, 256, 128))

    def swap_total(event):
        group, first, count = cuts[event]
        kind = side if group == 0 else other
        spot = pl.ds(first, count)
        return pltpu.make_async_remote_copy(
            src_ref=give_total_ref.at[group, spot],
            dst_ref=got_total_ref.at[kind, spot],
            send_sem=total_send.at[event],
            recv_sem=total_recv.at[event],
            device_id=partner,
            device_id_type=MESH,
        )

    def hand_over(event):
        group, first, count = cuts[event]
        spot = pl.ds(first, count)
        give_total_ref[group, spot, :] = total_ref[group, spot, far_cols].astype(jnp.bfloat16)
        go(swap_total(event))

    keep = flag_ref[0] == 0
    sign = jnp.where(keep, 1.0, -1.0)
    twice = jnp.where(keep, 0.0, 2.0)
    saves = []

    def finish(group, first_row, count):
        kind = side if group == 0 else other
        kind_part = near_part if group == 0 else far_part
        for tile_row in range(first_row // PART, (first_row + count) // PART):
            spot = slice(tile_row * PART, (tile_row + 1) * PART)
            if group == 0:
                start = band_ref[tile_row, :, near_cols]
            else:
                first = tile_row * TILE + kind * PART
                down = lax.broadcasted_iota(jnp.int32, (PART, half_wide), 0) + (row * wide + first)
                across = lax.broadcasted_iota(jnp.int32, (PART, half_wide), 1) + col * half_wide
                shift = jnp.where(down == across, shift_ref[0], jnp.float32(0.0))
                start = shift + scale_ref[0] * (core_ref[tile_row, far_part] + got_ref[tile_row])
            square = total_ref[group, spot, near_cols] + got_total_ref[kind, spot, :].astype(jnp.float32)
            out_ref[tile_row, kind_part] = sign * square + twice * start
        tile_rows = pl.ds(first_row // PART, count // PART)
        save = pltpu.make_async_copy(
            out_ref.at[tile_rows, kind_part], out_hbm.at[tile_rows, kind_part], save_sem.at[len(saves)]
        )
        save.start()
        saves.append(save)

    mine.wait()
    for dz in range(RING):
        core_copy(dz).wait_recv()
    for job in (0, 1):
        multiply(job, 0)
    pass_on(3)
    start_job(5)
    for job in (2, 3):
        multiply(job, 0)
    for job in (0, 1):
        far_landed(job)
        for dx in (3, 1, 2):
            multiply(job, dx)
    for dx in (3, 1):
        multiply(2, dx)
    far_landed(2)
    multiply(2, 2)
    for dx in (3, 1):
        multiply(3, dx)
    far_landed(3)
    multiply(3, 2)
    hand_over(0)
    pass_on(4)
    for dx in (0, 3, 1):
        multiply(4, dx)
    pair.wait_recv()
    for tile_row in range(BS):
        xc_ref[pl.ds(pl.multiple_of(tile_row * TILE + other * PART, PART), PART), :] = got_ref[tile_row]
    save_xc = pltpu.make_async_copy(xc_ref, xc_hbm, load_sem.at[1])
    save_xc.start()
    multiply(5, 0)
    far_landed(4)
    multiply(4, 2)
    hand_over(1)
    pass_on(5)
    for dx in (3, 1):
        multiply(5, dx)
    swap_total(0).wait_recv()
    finish(0, 0, 256)
    far_landed(5)
    multiply(5, 2)
    hand_over(2)
    finish(0, 256, 128)
    swap_total(1).wait_recv()
    finish(1, 0, 256)
    swap_total(2).wait_recv()
    finish(1, 256, 128)
    for copy in started:
        copy.wait_send()
    rest = landed_ref.at[pl.ds(0, DEVICES - 1)]
    pltpu.make_async_copy(rest, rest, all_send.at[1]).wait()
    save_rho.wait()
    save_xc.wait()
    for save in saves:
        save.wait()


def whole(shift, scale, flag, count, weights, tiles, density, basis, core_matrix):
    dma = pltpu.SemaphoreType.DMA
    tall, wide = core_matrix.shape
    points, width = basis.shape
    vmem = pl.BlockSpec(memory_space=pltpu.VMEM)
    smem = pl.BlockSpec(memory_space=pltpu.SMEM)
    hbm = pl.BlockSpec(memory_space=pl.ANY)
    bf16, f32 = jnp.bfloat16, jnp.float32
    return pl.pallas_call(
        whole_kernel,
        name="whole_kernel",
        out_shape=(
            jax.ShapeDtypeStruct((1, points), f32),
            jax.ShapeDtypeStruct((tall, wide), f32),
            jax.ShapeDtypeStruct((BS, TILE, wide), f32),
        ),
        in_specs=[smem, smem, smem, smem, vmem, hbm, hbm, hbm, hbm],
        out_specs=(hbm, hbm, hbm),
        scratch_shapes=[
            pltpu.SMEM((BLK, DEVICES), jnp.int32),
            pltpu.VMEM((BLK, DEVICES), jnp.int32),
            pltpu.VMEM((BLK, DEVICES), jnp.int32),
            pltpu.SMEM((BLK, DEVICES), jnp.int32),
            pltpu.VMEM((1, points), f32),
            pltpu.VMEM((tall, wide), f32),
            pltpu.VMEM((BS, TILE, wide), f32),
            pltpu.VMEM((points, width), bf16),
            pltpu.VMEM((BS, TILE, wide), f32),
            pltpu.VMEM((width, points), bf16),
            pltpu.VMEM((width, points), bf16),
            pltpu.VMEM((BS * BS, PART, TILE), bf16),
            pltpu.VMEM((DEVICES, PART, TILE), bf16),
            pltpu.VMEM((2, width // 2, width), bf16),
            pltpu.VMEM((width, width), bf16),
            pltpu.VMEM((DEVICES, PART, TILE), bf16),
            pltpu.VMEM((DEVICES + 1, PART, TILE), f32),
            pltpu.VMEM((BS, PART, 2 * wide), f32),
            pltpu.VMEM((BS * PART, 2 * wide), bf16),
            pltpu.VMEM((2, BS * PART, wide), bf16),
            pltpu.VMEM((BS, PART, wide), jnp.int16),
            pltpu.VMEM((BS, PART, wide), jnp.int16),
            pltpu.VMEM((8, TILE), f32),
            pltpu.VMEM((8, TILE), f32),
            pltpu.VMEM((BS, PART, wide), f32),
            pltpu.VMEM((BS, PART, wide), f32),
            pltpu.VMEM((RING, RING, BS * PART, wide), bf16),
            pltpu.VMEM((RING, 2, BS * PART, 2 * wide), bf16),
            pltpu.VMEM((2, BS * PART, 2 * wide), f32),
            pltpu.VMEM((2, BS * PART, wide), bf16),
            pltpu.VMEM((2, BS * PART, wide), bf16),
            dma((6,)),
            dma((BS // 2,)),
            dma((BS // 2,)),
            dma((BS // 2,)),
            dma((3,)),
            dma((3,)),
            dma((3,)),
            dma((3,)),
            dma((2,)),
            dma((2,)),
            dma((2,)),
            dma((len(JOBS), RING, 2)),
            dma((len(JOBS), RING, 2)),
            dma((RING,)),
            dma((RING,)),
            dma((4,)),
            dma((RING, 2)),
            dma((RING, 2)),
            dma((RING,)),
            dma((RING,)),
            dma,
        ],
        compiler_params=pltpu.CompilerParams(
            collective_id=1, has_side_effects=True, vmem_limit_bytes=56 * 2**20
        ),
        cost_estimate=pl.CostEstimate(
            flops=4 * points * width * width + 2 * tall * wide * tall * 8, bytes_accessed=16 * 2**20, transcendentals=0
        ),
    )(shift, scale, flag, count, weights, tiles, density.reshape(BS, TILE, wide), basis, core_matrix.reshape(BS, TILE, wide))


def keep_kernel(*refs):
    count = (len(refs) - 1) // 3
    sems = refs[-1]
    loads, saves = [], []
    for i in range(count):
        source, target, held = refs[i], refs[count + i], refs[2 * count + i]
        loads.append(pltpu.make_async_copy(source, held, sems.at[0, i]))
        saves.append(pltpu.make_async_copy(held, target, sems.at[1, i]))
    for load in loads:
        load.start()
    for load, save in zip(loads, saves):
        load.wait()
        save.start()
    for save in saves:
        save.wait()


def kept(*arrays):
    hbm = pl.BlockSpec(memory_space=pl.ANY)
    return pl.pallas_call(
        keep_kernel,
        name="keep_kernel",
        out_shape=tuple(jax.ShapeDtypeStruct(a.shape, a.dtype) for a in arrays),
        in_specs=[hbm] * len(arrays),
        out_specs=(hbm,) * len(arrays),
        scratch_shapes=[pltpu.VMEM(a.shape, a.dtype) for a in arrays] + [pltpu.SemaphoreType.DMA((2, len(arrays)))],
    )(*arrays)


def body(
    basis_values,
    quad_weights,
    point_counts,
    basis_tiles,
    density,
    core_matrix,
    map_shift,
    map_scale,
    branch_flags,
):
    density_out, potential, purified = whole(
        map_shift,
        map_scale,
        branch_flags,
        point_counts,
        quad_weights,
        basis_tiles.T,
        density,
        basis_values[0],
        core_matrix,
    )
    return kept(density_out, potential, purified.reshape(core_matrix.shape))


def solution(mesh):
    placed = (
        P(("row", "col"), None, None),
        P(("row", "col"), None),
        P(("row", "col")),
        P(),
        P("row", "col"),
        P("row", "col"),
        P(),
        P(),
        P(),
    )
    return jax.shard_map(
        body,
        mesh=mesh,
        in_specs=placed,
        out_specs=(P(("row", "col"), None), P("row", "col"), P("row", "col")),
        check_vma=False,
    )
```

```python
import jax
import jax.numpy as jnp
from jax import lax
from jax.experimental import pallas as pl
from jax.experimental.pallas import tpu as pltpu
from jax.sharding import PartitionSpec as P

MESH = pl.DeviceIdType.MESH
TILE = 128
PART = TILE // 2
BLK = 8
BS = 6
RING = 4
COLS = 16
DEVICES = 128
STRIDE = 37
SLATER = (3.0 / 3.141592653589793) ** (1.0 / 3.0)

def potential_factor(values):
    return -SLATER * (values * values + 1.0) ** (1.0 / 6.0)


def turn(value, step):
    return lax.rem(value + (step % RING), RING)


def offset_device(row, col, half, count):
    step = lax.rem(count * STRIDE, DEVICES // 2)
    z, core = row // 2, lax.rem(row, 2)
    x, y = col // RING, lax.rem(col, RING)
    dx, dy = step // 16, lax.rem(step // 4, RING)
    dz, dcore = half + lax.rem(step // 2, 2) * 2, lax.rem(step, 2)
    there = lax.rem(z + dz, RING) * 2 + lax.rem(core + dcore, 2)
    return there, lax.rem(x + dx, RING) * RING + lax.rem(y + dy, RING)


CHUNK = 256
STEPS = 32767.0
JOBS = ((0, 64, 160), (0, 224, 160), (3, 64, 320), (1, 64, 320), (2, 64, 192), (2, 256, 128))


def greet_all(me):
    barrier = pltpu.get_barrier_semaphore()

    @pl.loop(1, DEVICES, unroll=8)
    def _(step):
        there = (me + step) & (DEVICES - 1)
        pl.semaphore_signal(
            barrier, inc=1, device_id=(there >> 4, there & (COLS - 1)), device_id_type=MESH
        )

    return barrier


def hop(place):
    position, part = place
    if position == 3:
        return 1, 0
    if position == 1:
        return -1, 0
    return (1, 3) if part == 0 else (-1, 1)


def whole_kernel(
    shift_ref,
    scale_ref,
    flag_ref,
    count_ref,
    weights_ref,
    tiles_hbm,
    dens_ref,
    basis_hbm,
    core_hbm,
    rho_hbm,
    xc_hbm,
    out_hbm,
    tiles_ref,
    tiles_vec,
    chain_vec,
    chain_ref,
    rho_ref,
    xc_ref,
    out_ref,
    basis_ref,
    core_ref,
    turned_ref,
    scaled_ref,
    both_ref,
    stage_ref,
    sub_ref,
    block_ref,
    landed_ref,
    sums_ref,
    band_ref,
    own_ref,
    depth_ref,
    give_core_ref,
    got_core_ref,
    give_most_ref,
    got_most_ref,
    give_ref,
    got_ref,
    early_ref,
    late_ref,
    piece_ref,
    cols_ref,
    total_ref,
    give_total_ref,
    got_total_ref,
    load_sem,
    in_send,
    in_recv,
    in_own,
    swap_send,
    swap_recv,
    total_send,
    total_recv,
    all_send,
    all_recv,
    in_halves,
    row_send,
    row_recv,
    y_send,
    y_recv,
    early_send,
    early_recv,
    late_send,
    late_recv,
    save_sem,
    col_send,
    col_recv,
    core_send,
    core_recv,
    own_sem,
):
    row, col = lax.axis_index("row"), lax.axis_index("col")
    slot, side = col // 2, lax.rem(col, 2)
    other = 1 - side
    me = row * COLS + col
    partner = (row, slot * 2 + other)
    load_basis = pltpu.make_async_copy(basis_hbm, basis_ref, load_sem.at[0])
    load_core = pltpu.make_async_copy(core_hbm, core_ref, load_sem.at[1])
    half_wide = core_hbm.shape[2]
    near_cols = pl.ds(pl.multiple_of(side * half_wide, half_wide), half_wide)
    far_cols = pl.ds(pl.multiple_of(other * half_wide, half_wide), half_wide)
    near_part = pl.ds(pl.multiple_of(side * PART, PART), PART)
    far_part = pl.ds(pl.multiple_of(other * PART, PART), PART)
    mine_core = pltpu.make_async_copy(core_hbm.at[:, near_part], band_ref.at[:, :, near_cols], load_sem.at[5])
    swap_core = pltpu.make_async_remote_copy(
        src_ref=give_core_ref,
        dst_ref=got_core_ref,
        send_sem=swap_send.at[0],
        recv_sem=swap_recv.at[0],
        device_id=partner,
        device_id_type=MESH,
    )
    swap_most = pltpu.make_async_remote_copy(
        src_ref=give_most_ref,
        dst_ref=got_most_ref,
        send_sem=swap_send.at[2],
        recv_sem=swap_recv.at[2],
        device_id=partner,
        device_id_type=MESH,
    )
    load_tiles = [
        pltpu.make_async_copy(tiles_hbm, tiles_ref, load_sem.at[2]),
        pltpu.make_async_copy(tiles_hbm, tiles_vec, load_sem.at[3]),
    ]
    for copy in load_tiles:
        copy.start()
    barrier = greet_all(me)
    for copy in load_tiles:
        copy.wait()

    pairs, mines = [], []
    for tile in range(BS // 2):
        cut = pl.ds(tile * TILE, TILE)
        spot = both_ref.at[pl.ds((side * (BS // 2) + tile) * BS, BS)]
        pairs.append(
            pltpu.make_async_remote_copy(
                src_ref=dens_ref.at[:, pl.ds(pl.multiple_of(other * PART, PART), PART), cut],
                dst_ref=spot,
                send_sem=in_send.at[tile],
                recv_sem=in_recv.at[tile],
                device_id=partner,
                device_id_type=MESH,
            )
        )
        mines.append(
            pltpu.make_async_copy(
                dens_ref.at[:, pl.ds(pl.multiple_of(side * PART, PART), PART), cut], spot, in_own.at[tile]
            )
        )
    for copy in mines:
        copy.start()
    pl.semaphore_wait(barrier, DEVICES - 1)
    for copy in pairs:
        copy.start()
    load_core.start()
    load_basis.start()
    mine_core.start()
    for copy in mines + pairs:
        copy.wait()

    depth_z, depth_core = row // 2, lax.rem(row, 2)
    spot_cols = pl.ds(pl.multiple_of(slot * TILE, TILE), TILE)

    def landing(half):
        first = (depth_z // 2) * 2 * TILE + depth_core * TILE + side * PART
        return sub_ref.at[half, pl.ds(pl.multiple_of(first, PART), PART), spot_cols]

    def stage(target):
        batch = target[0] * COLS + target[1]
        tile_row = tiles_ref[row, batch] - row * BS
        tile_col = tiles_ref[slot, batch] - slot * BS
        stage_ref[batch] = both_ref[jnp.clip(tile_col * BS + tile_row, 0, BS * BS - 1)]
        return batch

    for half in (0, 1):

        @pl.loop(1 - half, DEVICES // 2)
        def _(count, half=half):
            target = offset_device(row, col, half, count)
            batch = stage(target)
            pltpu.make_async_remote_copy(
                src_ref=stage_ref.at[batch],
                dst_ref=landing(half),
                send_sem=all_send.at[0],
                recv_sem=in_halves.at[half],
                device_id=target,
                device_id_type=MESH,
            ).start()

        if half == 0:
            stage((row, col))
            pltpu.make_async_copy(stage_ref.at[me], landing(0), in_halves.at[0]).start()

    key = (tiles_vec[pl.ds(row, 1), :] - row * BS) * BS + tiles_vec[pl.ds(slot, 1), :] - slot * BS
    across = jnp.broadcast_to(key, (DEVICES, DEVICES))
    down = across.T
    batch_down = lax.broadcasted_iota(jnp.int32, across.shape, 0)
    batch_across = lax.broadcasted_iota(jnp.int32, across.shape, 1)
    earlier = (down == across) & (batch_down < batch_across)
    prev = jnp.max(jnp.where(earlier, batch_down, -1), axis=0, keepdims=True)
    last = jnp.max(jnp.where(down == batch_across, batch_down, -1), axis=0, keepdims=True)
    chain_vec[...] = jnp.zeros_like(chain_vec)
    chain_vec[0:1, :] = jnp.where(prev < 0, DEVICES, prev)
    chain_vec[1:2, :] = jnp.where(last < 0, DEVICES, last)
    load_chain = pltpu.make_async_copy(chain_vec, chain_ref, load_sem.at[4])
    load_chain.start()

    load_core.wait()
    most = jnp.zeros((1, 1), jnp.float32)
    for tile_row in range(BS):
        strip_most = jnp.max(jnp.abs(core_ref[tile_row, far_part]), axis=0, keepdims=True)
        most = jnp.maximum(most, jnp.max(strip_most, axis=1, keepdims=True))
    most = jnp.maximum(most, 1e-30)
    give_most_ref[...] = jnp.broadcast_to(most, give_most_ref.shape)
    for tile_row in range(BS):
        steps = jnp.round(core_ref[tile_row, far_part] * (STEPS / most))
        give_core_ref[tile_row] = steps.astype(jnp.int32).astype(jnp.int16)

    points, width = basis_ref.shape
    load_basis.wait()

    @pl.loop(0, points // CHUNK)
    def _(step):
        first = pl.multiple_of(step * CHUNK, CHUNK)
        turned_ref[:, pl.ds(first, CHUNK)] = basis_ref[pl.ds(first, CHUNK), :].T

    def band(half, which):
        place = which * 2 + lax.rem(depth_z + half, 2)
        return pl.ds(pl.multiple_of(place * 2 * TILE, 2 * TILE), 2 * TILE)

    for half in (0, 1):
        landed_half = pltpu.make_async_copy(sub_ref.at[half], sub_ref.at[half], in_halves.at[half])
        landed_half.wait()
        if half == 1:
            swap_core.start()
            swap_most.start()

        @pl.loop(0, points // CHUNK)
        def _(step, half=half):
            cut = pl.ds(pl.multiple_of(step * CHUNK, CHUNK), CHUNK)
            mixed = jnp.dot(sub_ref[half], turned_ref[:, cut], preferred_element_type=jnp.float32)
            density = jnp.zeros((1, CHUNK), jnp.float32)
            for which in (0, 1):
                values = turned_ref[band(half, which), cut].astype(jnp.float32)
                part = mixed[which * 2 * TILE : (which + 1) * 2 * TILE]
                density += jnp.sum(part * values, axis=0, keepdims=True)
            if half == 0:
                rho_ref[:, cut] = density
                return
            density += rho_ref[:, cut]
            live = lax.broadcasted_iota(jnp.int32, density.shape, 1) + step * CHUNK < count_ref[0]
            density = jnp.where(live, density, jnp.float32(0.0))
            rho_ref[:, cut] = density
            factor = jnp.where(live, weights_ref[:, cut] * potential_factor(density), jnp.float32(0.0))
            scaled_ref[:, cut] = (factor * turned_ref[:, cut].astype(jnp.float32)).astype(jnp.bfloat16)

    def piece(target):
        there_row, there_col = target
        first = there_row * TILE + lax.rem(there_col, 2) * PART
        return block_ref.at[
            pl.ds(pl.multiple_of(first, PART), PART),
            pl.ds(pl.multiple_of(there_col // 2 * TILE, TILE), TILE),
        ]

    for half in (0, 1):
        bands = [band(half, 0), band(half, 1)]
        values = jnp.concatenate([turned_ref[spot, :] for spot in bands], axis=0)
        result = lax.dot_general(
            values, scaled_ref[...], (((1,), (1,)), ((), ())), preferred_element_type=jnp.float32
        ).astype(jnp.bfloat16)
        for which in (0, 1):
            block_ref[bands[which], :] = result[which * 2 * TILE : (which + 1) * 2 * TILE]

        @pl.loop(1 - half, DEVICES // 2)
        def _(count, half=half):
            target = offset_device(row, col, half, count)
            pltpu.make_async_remote_copy(
                src_ref=piece(target),
                dst_ref=landed_ref.at[me],
                send_sem=all_send.at[1],
                recv_sem=all_recv.at[1],
                device_id=target,
                device_id_type=MESH,
            ).start()

        if half == 0:
            pltpu.make_async_copy(piece((row, col)), landed_ref.at[me], all_recv.at[1]).start()

    sums_ref[DEVICES] = jnp.zeros((PART, TILE), jnp.float32)
    rest = stage_ref.at[pl.ds(0, DEVICES - 1)]
    pltpu.make_async_copy(rest, rest, all_send.at[0]).wait()
    load_chain.wait()
    save_rho = pltpu.make_async_copy(rho_ref, rho_hbm, load_sem.at[0])
    save_rho.start()
    pltpu.make_async_copy(landed_ref, landed_ref, all_recv.at[1]).wait()

    @pl.loop(0, DEVICES)
    def _(batch):
        sums_ref[batch] = sums_ref[chain_ref[0, batch]] + landed_ref[batch].astype(jnp.float32)

    def total(tile_row, tile):
        return sums_ref[chain_ref[1, tile_row * BS + tile]]

    mine_core.wait()
    swap_core.wait()
    swap_most.wait()
    most = got_most_ref[0:1, 0:1] / STEPS
    wide = BS * TILE
    for tile_row in range(BS):
        value = jnp.concatenate([total(tile_row, tile) for tile in range(BS)], axis=1)
        down = lax.broadcasted_iota(jnp.int32, value.shape, 0) + (row * wide + tile_row * TILE + side * PART)
        across = lax.broadcasted_iota(jnp.int32, value.shape, 1) + slot * wide
        shift = jnp.where(down == across, shift_ref[0], jnp.float32(0.0))
        band_ref[tile_row, :, far_cols] = got_core_ref[tile_row].astype(jnp.int32).astype(jnp.float32) * most
        start = shift + scale_ref[0] * (band_ref[tile_row] + value)
        band_ref[tile_row] = start
        spot = slice(tile_row * PART, (tile_row + 1) * PART)
        own_ref[spot, :] = start.astype(jnp.bfloat16)
        for depth in (0, 1):
            lanes = [start[:, tile * TILE + depth * PART : tile * TILE + (depth + 1) * PART] for tile in range(BS)]
            halves = jnp.concatenate(lanes, axis=1).astype(jnp.bfloat16)
            if tile_row == 0:
                early_ref[depth, 0] = halves
            else:
                depth_ref[depth, spot, :] = halves

    z, core = row // 2, lax.rem(row, 2)
    x, y = col // RING, lax.rem(col, RING)
    piece_rows = own_ref.shape[0]

    def device(axis, step):
        if axis == "x":
            return (row, turn(x, step) * RING + y)
        if axis == "y":
            return (row, x * RING + turn(y, step))
        if axis == "z":
            return (turn(z, step) * 2 + core, col)
        return (z * 2 + 1 - core, col)

    def piece_at(dx, dy):
        if dx == 0 and dy == 0:
            return depth_ref.at[side]
        return piece_ref.at[dx, dy]

    def y_copy(dy):
        step = -dy
        spot = pl.ds(PART, piece_rows - PART)
        return pltpu.make_async_remote_copy(
            src_ref=depth_ref.at[side if dy == 2 else other, spot],
            dst_ref=piece_ref.at[0, dy, spot],
            send_sem=y_send.at[dy],
            recv_sem=y_recv.at[dy],
            device_id=device("y", step),
            device_id_type=MESH,
        )

    def x_copy(job, dx, part=0):
        dy, first, count = JOBS[job]
        step, source = hop((dx, part))
        if dx == 2:
            first, count = first + part * (count // 2), count // 2
        spot = pl.ds(first, count)
        return pltpu.make_async_remote_copy(
            src_ref=piece_at(source, dy).at[spot],
            dst_ref=piece_ref.at[dx, dy].at[spot],
            send_sem=row_send.at[job, dx, part],
            recv_sem=row_recv.at[job, dx, part],
            device_id=device("x", step),
            device_id_type=MESH,
        )

    def early_copy(dx, part=0):
        step, source = hop((dx, part))
        kinds = pl.ds(part, 1) if dx == 2 else pl.ds(0, 2)
        return pltpu.make_async_remote_copy(
            src_ref=early_ref.at[kinds, source],
            dst_ref=early_ref.at[kinds, dx],
            send_sem=early_send.at[dx, part],
            recv_sem=early_recv.at[dx, part],
            device_id=device("x", step),
            device_id_type=MESH,
        )

    def late_copy(dy):
        return pltpu.make_async_remote_copy(
            src_ref=early_ref.at[side if dy == 2 else other],
            dst_ref=late_ref.at[dy],
            send_sem=late_send.at[dy],
            recv_sem=late_recv.at[dy],
            device_id=device("y", -dy),
            device_id_type=MESH,
        )

    def z_copy(dz, part=0):
        step, source = hop((dz, part))
        place = turn(z, source)
        src = own_ref if source == 0 else cols_ref.at[place, core]
        dst = cols_ref.at[place, core]
        if dz == 2:
            part_rows = pl.ds(part * (piece_rows // 2), piece_rows // 2)
            src, dst = src.at[part_rows], dst.at[part_rows]
        return pltpu.make_async_remote_copy(
            src_ref=src,
            dst_ref=dst,
            send_sem=col_send.at[dz, part],
            recv_sem=col_recv.at[dz, part],
            device_id=device("z", step),
            device_id_type=MESH,
        )

    def core_copy(dz):
        place = turn(z, dz)
        return pltpu.make_async_remote_copy(
            src_ref=own_ref if dz == 0 else cols_ref.at[place, core],
            dst_ref=cols_ref.at[place, core],
            send_sem=core_send.at[dz],
            recv_sem=core_recv.at[dz],
            device_id=device("core", 1),
            device_id_type=MESH,
        )

    started = []

    def go(copy):
        copy.start()
        started.append(copy)

    def start_job(job):
        for dx in (3, 1):
            go(x_copy(job, dx))

    def pass_on(job):
        for dx, part in ((3, 0), (1, 1)):
            x_copy(job, dx).wait_recv()
            go(x_copy(job, 2, part))

    def far_landed(job):
        for part in (0, 1):
            x_copy(job, 2, part).wait_recv()

    for dx in (3, 1):
        go(early_copy(dx))
    start_job(0)
    start_job(1)
    for dy in (3, 1, 2):
        go(y_copy(dy))
    for dz in (3, 1):
        go(z_copy(dz))
    go(core_copy(0))
    mine = pltpu.make_async_copy(own_ref, cols_ref.at[z, core], own_sem)
    mine.start()

    def strip(tile_row, half):
        found = [sums_ref[chain_ref[1, tile_row * BS + half * (BS // 2) + tile]] for tile in range(BS // 2)]
        return jnp.concatenate(found, axis=1)

    for tile_row in range(BS):
        give_ref[tile_row] = strip(tile_row, other).astype(jnp.bfloat16)
    pair = pltpu.make_async_remote_copy(
        src_ref=give_ref,
        dst_ref=got_ref,
        send_sem=swap_send.at[1],
        recv_sem=swap_recv.at[1],
        device_id=partner,
        device_id_type=MESH,
    )
    for tile_row in range(BS):
        xc_ref[pl.ds(pl.multiple_of(tile_row * TILE + side * PART, PART), PART), :] = strip(tile_row, side)

    for dx, part in ((3, 0), (1, 1)):
        early_copy(dx).wait_recv()
        go(early_copy(2, part))
    pass_on(0)
    y_copy(3).wait_recv()
    start_job(2)
    pass_on(1)
    y_copy(1).wait_recv()
    start_job(3)
    for dz, part in ((3, 0), (1, 1)):
        z_copy(dz).wait_recv()
        go(z_copy(2, part))
        go(core_copy(dz))
    for part in (0, 1):
        early_copy(2, part).wait_recv()
    for dy in (3, 1, 2):
        go(late_copy(dy))
    y_copy(2).wait_recv()
    go(pair)
    pass_on(2)
    start_job(4)
    for part in (0, 1):
        z_copy(2, part).wait_recv()
    go(core_copy(2))

    def multiply(job, dx):
        dy, first, count = JOBS[job]
        spot = pl.ds(first, count)
        there_x, there_y = turn(x, dx), turn(y, dy)
        factor = cols_ref[there_x, there_y // 2]
        product = jnp.dot(piece_at(dx, dy)[spot, :], factor, preferred_element_type=jnp.float32)
        group = dy % 2
        if dx == 0 and dy in (0, 3):
            total_ref[group, spot, :] = product
        else:
            total_ref[group, spot, :] += product

    def multiply_early(dy):
        group = dy % 2
        spot = pl.ds(0, PART)
        for dx in range(RING):
            there_x, there_y = turn(x, dx), turn(y, dy)
            factor = cols_ref[there_x, there_y // 2]
            values = early_ref[side, dx] if dy == 0 else late_ref[dy, dx]
            product = jnp.dot(values, factor, preferred_element_type=jnp.float32)
            if dx == 0 and dy in (0, 3):
                total_ref[group, spot, :] = product
            else:
                total_ref[group, spot, :] += product

    cuts = ((1, 0, 384), (0, 0, 256), (0, 256, 128))

    def swap_total(event):
        group, first, count = cuts[event]
        kind = side if group == 0 else other
        spot = pl.ds(first, count)
        return pltpu.make_async_remote_copy(
            src_ref=give_total_ref.at[group, spot],
            dst_ref=got_total_ref.at[kind, spot],
            send_sem=total_send.at[event],
            recv_sem=total_recv.at[event],
            device_id=partner,
            device_id_type=MESH,
        )

    def hand_over(event):
        group, first, count = cuts[event]
        spot = pl.ds(first, count)
        give_total_ref[group, spot, :] = total_ref[group, spot, far_cols].astype(jnp.bfloat16)
        go(swap_total(event))

    keep = flag_ref[0] == 0
    sign = jnp.where(keep, 1.0, -1.0)
    twice = jnp.where(keep, 0.0, 2.0)
    saves = []

    def finish(group, first_row, count):
        kind = side if group == 0 else other
        kind_part = near_part if group == 0 else far_part
        for tile_row in range(first_row // PART, (first_row + count) // PART):
            spot = slice(tile_row * PART, (tile_row + 1) * PART)
            if group == 0:
                start = band_ref[tile_row, :, near_cols]
            else:
                first = tile_row * TILE + kind * PART
                down = lax.broadcasted_iota(jnp.int32, (PART, half_wide), 0) + (row * wide + first)
                across = lax.broadcasted_iota(jnp.int32, (PART, half_wide), 1) + col * half_wide
                shift = jnp.where(down == across, shift_ref[0], jnp.float32(0.0))
                start = shift + scale_ref[0] * (core_ref[tile_row, far_part] + got_ref[tile_row].astype(jnp.float32))
            square = total_ref[group, spot, near_cols] + got_total_ref[kind, spot, :].astype(jnp.float32)
            out_ref[tile_row, kind_part] = sign * square + twice * start
        tile_rows = pl.ds(first_row // PART, count // PART)
        save = pltpu.make_async_copy(
            out_ref.at[tile_rows, kind_part], out_hbm.at[tile_rows, kind_part], save_sem.at[len(saves)]
        )
        save.start()
        saves.append(save)

    mine.wait()
    for dz in range(RING):
        core_copy(dz).wait_recv()
    for job in (0, 1):
        multiply(job, 0)
    pass_on(3)
    start_job(5)
    for job in (2, 3):
        multiply(job, 0)
    for job in (0, 1):
        far_landed(job)
        for dx in (3, 1, 2):
            multiply(job, dx)
    for dx in (3, 1):
        multiply(2, dx)
    far_landed(2)
    multiply(2, 2)
    for dx in (3, 1):
        multiply(3, dx)
    far_landed(3)
    multiply(3, 2)
    for dy in (3, 1):
        late_copy(dy).wait_recv()
        multiply_early(dy)
    hand_over(0)
    pass_on(4)
    multiply_early(0)
    late_copy(2).wait_recv()
    multiply_early(2)
    for dx in (0, 3, 1):
        multiply(4, dx)
    pair.wait_recv()
    for tile_row in range(BS):
        xc_ref[pl.ds(pl.multiple_of(tile_row * TILE + other * PART, PART), PART), :] = got_ref[tile_row].astype(jnp.float32)
    save_xc = pltpu.make_async_copy(xc_ref, xc_hbm, load_sem.at[1])
    save_xc.start()
    multiply(5, 0)
    far_landed(4)
    multiply(4, 2)
    hand_over(1)
    pass_on(5)
    for dx in (3, 1):
        multiply(5, dx)
    swap_total(0).wait_recv()
    finish(0, 0, 256)
    far_landed(5)
    multiply(5, 2)
    hand_over(2)
    finish(0, 256, 128)
    swap_total(1).wait_recv()
    finish(1, 0, 256)
    swap_total(2).wait_recv()
    finish(1, 256, 128)
    for copy in started:
        copy.wait_send()
    rest = landed_ref.at[pl.ds(0, DEVICES - 1)]
    pltpu.make_async_copy(rest, rest, all_send.at[1]).wait()
    save_rho.wait()
    save_xc.wait()
    for save in saves:
        save.wait()


def whole(shift, scale, flag, count, weights, tiles, density, basis, core_matrix):
    dma = pltpu.SemaphoreType.DMA
    tall, wide = core_matrix.shape
    points, width = basis.shape
    vmem = pl.BlockSpec(memory_space=pltpu.VMEM)
    smem = pl.BlockSpec(memory_space=pltpu.SMEM)
    hbm = pl.BlockSpec(memory_space=pl.ANY)
    bf16, f32 = jnp.bfloat16, jnp.float32
    return pl.pallas_call(
        whole_kernel,
        name="whole_kernel",
        out_shape=(
            jax.ShapeDtypeStruct((1, points), f32),
            jax.ShapeDtypeStruct((tall, wide), f32),
            jax.ShapeDtypeStruct((BS, TILE, wide), f32),
        ),
        in_specs=[smem, smem, smem, smem, vmem, hbm, hbm, hbm, hbm],
        out_specs=(hbm, hbm, hbm),
        scratch_shapes=[
            pltpu.SMEM((BLK, DEVICES), jnp.int32),
            pltpu.VMEM((BLK, DEVICES), jnp.int32),
            pltpu.VMEM((BLK, DEVICES), jnp.int32),
            pltpu.SMEM((BLK, DEVICES), jnp.int32),
            pltpu.VMEM((1, points), f32),
            pltpu.VMEM((tall, wide), f32),
            pltpu.VMEM((BS, TILE, wide), f32),
            pltpu.VMEM((points, width), bf16),
            pltpu.VMEM((BS, TILE, wide), f32),
            pltpu.VMEM((width, points), bf16),
            pltpu.VMEM((width, points), bf16),
            pltpu.VMEM((BS * BS, PART, TILE), bf16),
            pltpu.VMEM((DEVICES, PART, TILE), bf16),
            pltpu.VMEM((2, width // 2, width), bf16),
            pltpu.VMEM((width, width), bf16),
            pltpu.VMEM((DEVICES, PART, TILE), bf16),
            pltpu.VMEM((DEVICES + 1, PART, TILE), f32),
            pltpu.VMEM((BS, PART, 2 * wide), f32),
            pltpu.VMEM((BS * PART, 2 * wide), bf16),
            pltpu.VMEM((2, BS * PART, wide), bf16),
            pltpu.VMEM((BS, PART, wide), jnp.int16),
            pltpu.VMEM((BS, PART, wide), jnp.int16),
            pltpu.VMEM((8, TILE), f32),
            pltpu.VMEM((8, TILE), f32),
            pltpu.VMEM((BS, PART, wide), bf16),
            pltpu.VMEM((BS, PART, wide), bf16),
            pltpu.VMEM((2, RING, PART, wide), bf16),
            pltpu.VMEM((RING, RING, PART, wide), bf16),
            pltpu.VMEM((RING, RING, BS * PART, wide), bf16),
            pltpu.VMEM((RING, 2, BS * PART, 2 * wide), bf16),
            pltpu.VMEM((2, BS * PART, 2 * wide), f32),
            pltpu.VMEM((2, BS * PART, wide), bf16),
            pltpu.VMEM((2, BS * PART, wide), bf16),
            dma((6,)),
            dma((BS // 2,)),
            dma((BS // 2,)),
            dma((BS // 2,)),
            dma((3,)),
            dma((3,)),
            dma((3,)),
            dma((3,)),
            dma((2,)),
            dma((2,)),
            dma((2,)),
            dma((len(JOBS), RING, 2)),
            dma((len(JOBS), RING, 2)),
            dma((RING,)),
            dma((RING,)),
            dma((RING, 2)),
            dma((RING, 2)),
            dma((RING,)),
            dma((RING,)),
            dma((4,)),
            dma((RING, 2)),
            dma((RING, 2)),
            dma((RING,)),
            dma((RING,)),
            dma,
        ],
        compiler_params=pltpu.CompilerParams(
            collective_id=1, has_side_effects=True, vmem_limit_bytes=56 * 2**20
        ),
        cost_estimate=pl.CostEstimate(
            flops=4 * points * width * width + 2 * tall * wide * tall * 8, bytes_accessed=16 * 2**20, transcendentals=0
        ),
    )(shift, scale, flag, count, weights, tiles, density.reshape(BS, TILE, wide), basis, core_matrix.reshape(BS, TILE, wide))


def keep_kernel(*refs):
    count = (len(refs) - 1) // 3
    sems = refs[-1]
    loads, saves = [], []
    for i in range(count):
        source, target, held = refs[i], refs[count + i], refs[2 * count + i]
        parts = 4 if source.shape[0] > 1 else 1
        size = source.shape[0] // parts
        for part in range(parts):
            spot = pl.ds(part * size, size)
            loads.append(pltpu.make_async_copy(source.at[spot], held.at[spot], sems.at[0, i, part]))
            saves.append(pltpu.make_async_copy(held.at[spot], target.at[spot], sems.at[1, i, part]))
    for load in loads:
        load.start()
    for load, save in zip(loads, saves):
        load.wait()
        save.start()
    for save in saves:
        save.wait()


def kept(*arrays):
    hbm = pl.BlockSpec(memory_space=pl.ANY)
    return pl.pallas_call(
        keep_kernel,
        name="keep_kernel",
        out_shape=tuple(jax.ShapeDtypeStruct(a.shape, a.dtype) for a in arrays),
        in_specs=[hbm] * len(arrays),
        out_specs=(hbm,) * len(arrays),
        scratch_shapes=[pltpu.VMEM(a.shape, a.dtype) for a in arrays] + [pltpu.SemaphoreType.DMA((2, len(arrays), 4))],
    )(*arrays)


def body(
    basis_values,
    quad_weights,
    point_counts,
    basis_tiles,
    density,
    core_matrix,
    map_shift,
    map_scale,
    branch_flags,
):
    density_out, potential, purified = whole(
        map_shift,
        map_scale,
        branch_flags,
        point_counts,
        quad_weights,
        basis_tiles.T,
        density,
        basis_values[0],
        core_matrix,
    )
    return kept(density_out, potential, purified.reshape(core_matrix.shape))


def solution(mesh):
    placed = (
        P(("row", "col"), None, None),
        P(("row", "col"), None),
        P(("row", "col")),
        P(),
        P("row", "col"),
        P("row", "col"),
        P(),
        P(),
        P(),
    )
    return jax.shard_map(
        body,
        mesh=mesh,
        in_specs=placed,
        out_specs=(P(("row", "col"), None), P("row", "col"), P("row", "col")),
        check_vma=False,
    )
```

```python
import jax
import jax.numpy as jnp
from jax import lax
from jax.experimental import pallas as pl
from jax.experimental.pallas import tpu as pltpu
from jax.sharding import PartitionSpec as P

MESH = pl.DeviceIdType.MESH
TILE = 128
PART = TILE // 2
BLK = 8
BS = 6
RING = 4
COLS = 16
DEVICES = 128
STRIDE = 37
SLATER = (3.0 / 3.141592653589793) ** (1.0 / 3.0)

def potential_factor(values):
    return -SLATER * (values * values + 1.0) ** (1.0 / 6.0)


def turn(value, step):
    return lax.rem(value + (step % RING), RING)


def offset_device(row, col, half, count):
    step = lax.rem(count * STRIDE, DEVICES // 2)
    z, core = row // 2, lax.rem(row, 2)
    x, y = col // RING, lax.rem(col, RING)
    dx, dy = step // 16, lax.rem(step // 4, RING)
    dz, dcore = half + lax.rem(step // 2, 2) * 2, lax.rem(step, 2)
    there = lax.rem(z + dz, RING) * 2 + lax.rem(core + dcore, 2)
    return there, lax.rem(x + dx, RING) * RING + lax.rem(y + dy, RING)


CHUNK = 256
STEPS = 32767.0
JOBS = ((0, 64, 160), (0, 224, 160), (3, 64, 320), (1, 64, 320), (2, 64, 192), (2, 256, 128))


def greet_all(me):
    barrier = pltpu.get_barrier_semaphore()

    @pl.loop(1, DEVICES, unroll=8)
    def _(step):
        there = (me + step) & (DEVICES - 1)
        pl.semaphore_signal(
            barrier, inc=1, device_id=(there >> 4, there & (COLS - 1)), device_id_type=MESH
        )

    return barrier


def hop(place):
    position, part = place
    if position == 3:
        return 1, 0
    if position == 1:
        return -1, 0
    return (1, 3) if part == 0 else (-1, 1)


def whole_kernel(
    shift_ref,
    scale_ref,
    flag_ref,
    count_ref,
    weights_ref,
    tiles_hbm,
    dens_ref,
    basis_hbm,
    core_hbm,
    rho_hbm,
    xc_hbm,
    out_hbm,
    tiles_ref,
    tiles_vec,
    chain_vec,
    chain_ref,
    rho_ref,
    xc_ref,
    out_ref,
    basis_ref,
    core_ref,
    turned_ref,
    scaled_ref,
    both_ref,
    stage_ref,
    sub_ref,
    block_ref,
    landed_ref,
    sums_ref,
    band_ref,
    own_ref,
    depth_ref,
    give_core_ref,
    got_core_ref,
    give_most_ref,
    got_most_ref,
    give_ref,
    got_ref,
    early_ref,
    late_ref,
    piece_ref,
    cols_ref,
    total_ref,
    give_total_ref,
    got_total_ref,
    load_sem,
    in_send,
    in_recv,
    in_own,
    swap_send,
    swap_recv,
    total_send,
    total_recv,
    all_send,
    all_recv,
    in_halves,
    row_send,
    row_recv,
    y_send,
    y_recv,
    early_send,
    early_recv,
    late_send,
    late_recv,
    save_sem,
    col_send,
    col_recv,
    core_send,
    core_recv,
    own_sem,
):
    row, col = lax.axis_index("row"), lax.axis_index("col")
    slot, side = col // 2, lax.rem(col, 2)
    other = 1 - side
    me = row * COLS + col
    partner = (row, slot * 2 + other)
    load_basis = pltpu.make_async_copy(basis_hbm, basis_ref, load_sem.at[0])
    load_core = pltpu.make_async_copy(core_hbm, core_ref, load_sem.at[1])
    half_wide = core_hbm.shape[2]
    near_cols = pl.ds(pl.multiple_of(side * half_wide, half_wide), half_wide)
    far_cols = pl.ds(pl.multiple_of(other * half_wide, half_wide), half_wide)
    near_part = pl.ds(pl.multiple_of(side * PART, PART), PART)
    far_part = pl.ds(pl.multiple_of(other * PART, PART), PART)
    mine_core = pltpu.make_async_copy(core_hbm.at[:, near_part], band_ref.at[:, :, near_cols], load_sem.at[5])
    swap_core = pltpu.make_async_remote_copy(
        src_ref=give_core_ref,
        dst_ref=got_core_ref,
        send_sem=swap_send.at[0],
        recv_sem=swap_recv.at[0],
        device_id=partner,
        device_id_type=MESH,
    )
    swap_most = pltpu.make_async_remote_copy(
        src_ref=give_most_ref,
        dst_ref=got_most_ref,
        send_sem=swap_send.at[2],
        recv_sem=swap_recv.at[2],
        device_id=partner,
        device_id_type=MESH,
    )
    load_tiles = [
        pltpu.make_async_copy(tiles_hbm, tiles_ref, load_sem.at[2]),
        pltpu.make_async_copy(tiles_hbm, tiles_vec, load_sem.at[3]),
    ]
    for copy in load_tiles:
        copy.start()
    barrier = greet_all(me)
    for copy in load_tiles:
        copy.wait()

    pairs, mines = [], []
    for tile in range(BS // 2):
        cut = pl.ds(tile * TILE, TILE)
        spot = both_ref.at[pl.ds((side * (BS // 2) + tile) * BS, BS)]
        pairs.append(
            pltpu.make_async_remote_copy(
                src_ref=dens_ref.at[:, pl.ds(pl.multiple_of(other * PART, PART), PART), cut],
                dst_ref=spot,
                send_sem=in_send.at[tile],
                recv_sem=in_recv.at[tile],
                device_id=partner,
                device_id_type=MESH,
            )
        )
        mines.append(
            pltpu.make_async_copy(
                dens_ref.at[:, pl.ds(pl.multiple_of(side * PART, PART), PART), cut], spot, in_own.at[tile]
            )
        )
    for copy in mines:
        copy.start()
    pl.semaphore_wait(barrier, DEVICES - 1)
    for copy in pairs:
        copy.start()
    load_core.start()
    load_basis.start()
    mine_core.start()
    for copy in mines + pairs:
        copy.wait()

    depth_z, depth_core = row // 2, lax.rem(row, 2)
    spot_cols = pl.ds(pl.multiple_of(slot * TILE, TILE), TILE)

    def landing(half):
        first = (depth_z // 2) * 2 * TILE + depth_core * TILE + side * PART
        return sub_ref.at[half, pl.ds(pl.multiple_of(first, PART), PART), spot_cols]

    def stage(target):
        batch = target[0] * COLS + target[1]
        tile_row = tiles_ref[row, batch] - row * BS
        tile_col = tiles_ref[slot, batch] - slot * BS
        stage_ref[batch] = both_ref[jnp.clip(tile_col * BS + tile_row, 0, BS * BS - 1)]
        return batch

    for half in (0, 1):

        @pl.loop(1 - half, DEVICES // 2, unroll=4)
        def _(count, half=half):
            target = offset_device(row, col, half, count)
            batch = stage(target)
            pltpu.make_async_remote_copy(
                src_ref=stage_ref.at[batch],
                dst_ref=landing(half),
                send_sem=all_send.at[0],
                recv_sem=in_halves.at[half],
                device_id=target,
                device_id_type=MESH,
            ).start()

        if half == 0:
            stage((row, col))
            pltpu.make_async_copy(stage_ref.at[me], landing(0), in_halves.at[0]).start()

    key = (tiles_vec[pl.ds(row, 1), :] - row * BS) * BS + tiles_vec[pl.ds(slot, 1), :] - slot * BS
    across = jnp.broadcast_to(key, (DEVICES, DEVICES))
    down = across.T
    batch_down = lax.broadcasted_iota(jnp.int32, across.shape, 0)
    batch_across = lax.broadcasted_iota(jnp.int32, across.shape, 1)
    earlier = (down == across) & (batch_down < batch_across)
    prev = jnp.max(jnp.where(earlier, batch_down, -1), axis=0, keepdims=True)
    last = jnp.max(jnp.where(down == batch_across, batch_down, -1), axis=0, keepdims=True)
    chain_vec[...] = jnp.zeros_like(chain_vec)
    chain_vec[0:1, :] = jnp.where(prev < 0, DEVICES, prev)
    chain_vec[1:2, :] = jnp.where(last < 0, DEVICES, last)
    load_chain = pltpu.make_async_copy(chain_vec, chain_ref, load_sem.at[4])
    load_chain.start()

    load_core.wait()
    most = jnp.zeros((1, 1), jnp.float32)
    for tile_row in range(BS):
        strip_most = jnp.max(jnp.abs(core_ref[tile_row, far_part]), axis=0, keepdims=True)
        most = jnp.maximum(most, jnp.max(strip_most, axis=1, keepdims=True))
    most = jnp.maximum(most, 1e-30)
    give_most_ref[...] = jnp.broadcast_to(most, give_most_ref.shape)
    for tile_row in range(BS):
        steps = jnp.round(core_ref[tile_row, far_part] * (STEPS / most))
        give_core_ref[tile_row] = steps.astype(jnp.int32).astype(jnp.int16)

    points, width = basis_ref.shape
    load_basis.wait()

    @pl.loop(0, points // CHUNK)
    def _(step):
        first = pl.multiple_of(step * CHUNK, CHUNK)
        turned_ref[:, pl.ds(first, CHUNK)] = basis_ref[pl.ds(first, CHUNK), :].T

    def band(half, which):
        place = which * 2 + lax.rem(depth_z + half, 2)
        return pl.ds(pl.multiple_of(place * 2 * TILE, 2 * TILE), 2 * TILE)

    for half in (0, 1):
        landed_half = pltpu.make_async_copy(sub_ref.at[half], sub_ref.at[half], in_halves.at[half])
        landed_half.wait()
        if half == 1:
            swap_core.start()
            swap_most.start()

        @pl.loop(0, points // CHUNK)
        def _(step, half=half):
            cut = pl.ds(pl.multiple_of(step * CHUNK, CHUNK), CHUNK)
            mixed = jnp.dot(sub_ref[half], turned_ref[:, cut], preferred_element_type=jnp.float32)
            density = jnp.zeros((1, CHUNK), jnp.float32)
            for which in (0, 1):
                values = turned_ref[band(half, which), cut].astype(jnp.float32)
                part = mixed[which * 2 * TILE : (which + 1) * 2 * TILE]
                density += jnp.sum(part * values, axis=0, keepdims=True)
            if half == 0:
                rho_ref[:, cut] = density
                return
            density += rho_ref[:, cut]
            live = lax.broadcasted_iota(jnp.int32, density.shape, 1) + step * CHUNK < count_ref[0]
            density = jnp.where(live, density, jnp.float32(0.0))
            rho_ref[:, cut] = density
            factor = jnp.where(live, weights_ref[:, cut] * potential_factor(density), jnp.float32(0.0))
            scaled_ref[:, cut] = (factor * turned_ref[:, cut].astype(jnp.float32)).astype(jnp.bfloat16)

    def piece(target):
        there_row, there_col = target
        first = there_row * TILE + lax.rem(there_col, 2) * PART
        return block_ref.at[
            pl.ds(pl.multiple_of(first, PART), PART),
            pl.ds(pl.multiple_of(there_col // 2 * TILE, TILE), TILE),
        ]

    for half in (0, 1):
        bands = [band(half, 0), band(half, 1)]
        values = jnp.concatenate([turned_ref[spot, :] for spot in bands], axis=0)
        result = lax.dot_general(
            values, scaled_ref[...], (((1,), (1,)), ((), ())), preferred_element_type=jnp.float32
        ).astype(jnp.bfloat16)
        for which in (0, 1):
            block_ref[bands[which], :] = result[which * 2 * TILE : (which + 1) * 2 * TILE]

        @pl.loop(1 - half, DEVICES // 2, unroll=4)
        def _(count, half=half):
            target = offset_device(row, col, half, count)
            pltpu.make_async_remote_copy(
                src_ref=piece(target),
                dst_ref=landed_ref.at[me],
                send_sem=all_send.at[1],
                recv_sem=all_recv.at[1],
                device_id=target,
                device_id_type=MESH,
            ).start()

        if half == 0:
            pltpu.make_async_copy(piece((row, col)), landed_ref.at[me], all_recv.at[1]).start()

    sums_ref[DEVICES] = jnp.zeros((PART, TILE), jnp.float32)
    rest = stage_ref.at[pl.ds(0, DEVICES - 1)]
    pltpu.make_async_copy(rest, rest, all_send.at[0]).wait()
    load_chain.wait()
    save_rho = pltpu.make_async_copy(rho_ref, rho_hbm, load_sem.at[0])
    save_rho.start()
    pltpu.make_async_copy(landed_ref, landed_ref, all_recv.at[1]).wait()

    @pl.loop(0, DEVICES, unroll=4)
    def _(batch):
        sums_ref[batch] = sums_ref[chain_ref[0, batch]] + landed_ref[batch].astype(jnp.float32)

    def total(tile_row, tile):
        return sums_ref[chain_ref[1, tile_row * BS + tile]]

    mine_core.wait()
    swap_core.wait()
    swap_most.wait()
    most = got_most_ref[0:1, 0:1] / STEPS
    wide = BS * TILE
    for tile_row in range(BS):
        value = jnp.concatenate([total(tile_row, tile) for tile in range(BS)], axis=1)
        down = lax.broadcasted_iota(jnp.int32, value.shape, 0) + (row * wide + tile_row * TILE + side * PART)
        across = lax.broadcasted_iota(jnp.int32, value.shape, 1) + slot * wide
        shift = jnp.where(down == across, shift_ref[0], jnp.float32(0.0))
        band_ref[tile_row, :, far_cols] = got_core_ref[tile_row].astype(jnp.int32).astype(jnp.float32) * most
        start = shift + scale_ref[0] * (band_ref[tile_row] + value)
        band_ref[tile_row] = start
        spot = slice(tile_row * PART, (tile_row + 1) * PART)
        own_ref[spot, :] = start.astype(jnp.bfloat16)
        for depth in (0, 1):
            lanes = [start[:, tile * TILE + depth * PART : tile * TILE + (depth + 1) * PART] for tile in range(BS)]
            halves = jnp.concatenate(lanes, axis=1).astype(jnp.bfloat16)
            if tile_row == 0:
                early_ref[depth, 0] = halves
            else:
                depth_ref[depth, spot, :] = halves

    z, core = row // 2, lax.rem(row, 2)
    x, y = col // RING, lax.rem(col, RING)
    piece_rows = own_ref.shape[0]

    def device(axis, step):
        if axis == "x":
            return (row, turn(x, step) * RING + y)
        if axis == "y":
            return (row, x * RING + turn(y, step))
        if axis == "z":
            return (turn(z, step) * 2 + core, col)
        return (z * 2 + 1 - core, col)

    def piece_at(dx, dy):
        if dx == 0 and dy == 0:
            return depth_ref.at[side]
        return piece_ref.at[dx, dy]

    def y_copy(dy):
        step = -dy
        spot = pl.ds(PART, piece_rows - PART)
        return pltpu.make_async_remote_copy(
            src_ref=depth_ref.at[side if dy == 2 else other, spot],
            dst_ref=piece_ref.at[0, dy, spot],
            send_sem=y_send.at[dy],
            recv_sem=y_recv.at[dy],
            device_id=device("y", step),
            device_id_type=MESH,
        )

    def x_copy(job, dx, part=0):
        dy, first, count = JOBS[job]
        step, source = hop((dx, part))
        if dx == 2:
            first, count = first + part * (count // 2), count // 2
        spot = pl.ds(first, count)
        return pltpu.make_async_remote_copy(
            src_ref=piece_at(source, dy).at[spot],
            dst_ref=piece_ref.at[dx, dy].at[spot],
            send_sem=row_send.at[job, dx, part],
            recv_sem=row_recv.at[job, dx, part],
            device_id=device("x", step),
            device_id_type=MESH,
        )

    def early_copy(dx, part=0):
        step, source = hop((dx, part))
        kinds = pl.ds(part, 1) if dx == 2 else pl.ds(0, 2)
        return pltpu.make_async_remote_copy(
            src_ref=early_ref.at[kinds, source],
            dst_ref=early_ref.at[kinds, dx],
            send_sem=early_send.at[dx, part],
            recv_sem=early_recv.at[dx, part],
            device_id=device("x", step),
            device_id_type=MESH,
        )

    def late_copy(dy):
        return pltpu.make_async_remote_copy(
            src_ref=early_ref.at[side if dy == 2 else other],
            dst_ref=late_ref.at[dy],
            send_sem=late_send.at[dy],
            recv_sem=late_recv.at[dy],
            device_id=device("y", -dy),
            device_id_type=MESH,
        )

    def z_copy(dz, part=0):
        step, source = hop((dz, part))
        place = turn(z, source)
        src = own_ref if source == 0 else cols_ref.at[place, core]
        dst = cols_ref.at[place, core]
        if dz == 2:
            part_rows = pl.ds(part * (piece_rows // 2), piece_rows // 2)
            src, dst = src.at[part_rows], dst.at[part_rows]
        return pltpu.make_async_remote_copy(
            src_ref=src,
            dst_ref=dst,
            send_sem=col_send.at[dz, part],
            recv_sem=col_recv.at[dz, part],
            device_id=device("z", step),
            device_id_type=MESH,
        )

    def core_copy(dz):
        place = turn(z, dz)
        return pltpu.make_async_remote_copy(
            src_ref=own_ref if dz == 0 else cols_ref.at[place, core],
            dst_ref=cols_ref.at[place, core],
            send_sem=core_send.at[dz],
            recv_sem=core_recv.at[dz],
            device_id=device("core", 1),
            device_id_type=MESH,
        )

    started = []

    def go(copy):
        copy.start()
        started.append(copy)

    def start_job(job):
        for dx in (3, 1):
            go(x_copy(job, dx))

    def pass_on(job):
        for dx, part in ((3, 0), (1, 1)):
            x_copy(job, dx).wait_recv()
            go(x_copy(job, 2, part))

    def far_landed(job):
        for part in (0, 1):
            x_copy(job, 2, part).wait_recv()

    for dx in (3, 1):
        go(early_copy(dx))
    start_job(0)
    start_job(1)
    for dy in (3, 1, 2):
        go(y_copy(dy))
    for dz in (3, 1):
        go(z_copy(dz))
    go(core_copy(0))
    mine = pltpu.make_async_copy(own_ref, cols_ref.at[z, core], own_sem)
    mine.start()

    def strip(tile_row, half):
        found = [sums_ref[chain_ref[1, tile_row * BS + half * (BS // 2) + tile]] for tile in range(BS // 2)]
        return jnp.concatenate(found, axis=1)

    for tile_row in range(BS):
        give_ref[tile_row] = strip(tile_row, other).astype(jnp.bfloat16)
    pair = pltpu.make_async_remote_copy(
        src_ref=give_ref,
        dst_ref=got_ref,
        send_sem=swap_send.at[1],
        recv_sem=swap_recv.at[1],
        device_id=partner,
        device_id_type=MESH,
    )
    for tile_row in range(BS):
        xc_ref[pl.ds(pl.multiple_of(tile_row * TILE + side * PART, PART), PART), :] = strip(tile_row, side)

    for dx, part in ((3, 0), (1, 1)):
        early_copy(dx).wait_recv()
        go(early_copy(2, part))
    pass_on(0)
    y_copy(3).wait_recv()
    start_job(2)
    pass_on(1)
    y_copy(1).wait_recv()
    start_job(3)
    for dz, part in ((3, 0), (1, 1)):
        z_copy(dz).wait_recv()
        go(z_copy(2, part))
        go(core_copy(dz))
    for part in (0, 1):
        early_copy(2, part).wait_recv()
    for dy in (3, 1, 2):
        go(late_copy(dy))
    y_copy(2).wait_recv()
    go(pair)
    pass_on(2)
    start_job(4)
    for part in (0, 1):
        z_copy(2, part).wait_recv()
    go(core_copy(2))

    def multiply(job, dx):
        dy, first, count = JOBS[job]
        spot = pl.ds(first, count)
        there_x, there_y = turn(x, dx), turn(y, dy)
        factor = cols_ref[there_x, there_y // 2]
        product = jnp.dot(piece_at(dx, dy)[spot, :], factor, preferred_element_type=jnp.float32)
        group = dy % 2
        if dx == 0 and dy in (0, 3):
            total_ref[group, spot, :] = product
        else:
            total_ref[group, spot, :] += product

    def multiply_early(dy):
        group = dy % 2
        spot = pl.ds(0, PART)
        for dx in range(RING):
            there_x, there_y = turn(x, dx), turn(y, dy)
            factor = cols_ref[there_x, there_y // 2]
            values = early_ref[side, dx] if dy == 0 else late_ref[dy, dx]
            product = jnp.dot(values, factor, preferred_element_type=jnp.float32)
            if dx == 0 and dy in (0, 3):
                total_ref[group, spot, :] = product
            else:
                total_ref[group, spot, :] += product

    cuts = ((1, 0, 384), (0, 0, 256), (0, 256, 128))

    def swap_total(event):
        group, first, count = cuts[event]
        kind = side if group == 0 else other
        spot = pl.ds(first, count)
        return pltpu.make_async_remote_copy(
            src_ref=give_total_ref.at[group, spot],
            dst_ref=got_total_ref.at[kind, spot],
            send_sem=total_send.at[event],
            recv_sem=total_recv.at[event],
            device_id=partner,
            device_id_type=MESH,
        )

    def hand_over(event):
        group, first, count = cuts[event]
        spot = pl.ds(first, count)
        give_total_ref[group, spot, :] = total_ref[group, spot, far_cols].astype(jnp.bfloat16)
        go(swap_total(event))

    keep = flag_ref[0] == 0
    sign = jnp.where(keep, 1.0, -1.0)
    twice = jnp.where(keep, 0.0, 2.0)
    saves = []

    def finish(group, first_row, count):
        kind = side if group == 0 else other
        kind_part = near_part if group == 0 else far_part
        for tile_row in range(first_row // PART, (first_row + count) // PART):
            spot = slice(tile_row * PART, (tile_row + 1) * PART)
            if group == 0:
                start = band_ref[tile_row, :, near_cols]
            else:
                first = tile_row * TILE + kind * PART
                down = lax.broadcasted_iota(jnp.int32, (PART, half_wide), 0) + (row * wide + first)
                across = lax.broadcasted_iota(jnp.int32, (PART, half_wide), 1) + col * half_wide
                shift = jnp.where(down == across, shift_ref[0], jnp.float32(0.0))
                start = shift + scale_ref[0] * (core_ref[tile_row, far_part] + got_ref[tile_row].astype(jnp.float32))
            square = total_ref[group, spot, near_cols] + got_total_ref[kind, spot, :].astype(jnp.float32)
            out_ref[tile_row, kind_part] = sign * square + twice * start
        tile_rows = pl.ds(first_row // PART, count // PART)
        save = pltpu.make_async_copy(
            out_ref.at[tile_rows, kind_part], out_hbm.at[tile_rows, kind_part], save_sem.at[len(saves)]
        )
        save.start()
        saves.append(save)

    mine.wait()
    for dz in range(RING):
        core_copy(dz).wait_recv()
    for job in (0, 1):
        multiply(job, 0)
    pass_on(3)
    start_job(5)
    for job in (2, 3):
        multiply(job, 0)
    for job in (0, 1):
        far_landed(job)
        for dx in (3, 1, 2):
            multiply(job, dx)
    for dx in (3, 1):
        multiply(2, dx)
    far_landed(2)
    multiply(2, 2)
    for dx in (3, 1):
        multiply(3, dx)
    far_landed(3)
    multiply(3, 2)
    for dy in (3, 1):
        late_copy(dy).wait_recv()
        multiply_early(dy)
    hand_over(0)
    pass_on(4)
    multiply_early(0)
    late_copy(2).wait_recv()
    multiply_early(2)
    for dx in (0, 3, 1):
        multiply(4, dx)
    pair.wait_recv()
    for tile_row in range(BS):
        xc_ref[pl.ds(pl.multiple_of(tile_row * TILE + other * PART, PART), PART), :] = got_ref[tile_row].astype(jnp.float32)
    save_xc = pltpu.make_async_copy(xc_ref, xc_hbm, load_sem.at[1])
    save_xc.start()
    multiply(5, 0)
    far_landed(4)
    multiply(4, 2)
    hand_over(1)
    pass_on(5)
    for dx in (3, 1):
        multiply(5, dx)
    swap_total(0).wait_recv()
    finish(0, 0, 256)
    far_landed(5)
    multiply(5, 2)
    hand_over(2)
    finish(0, 256, 128)
    swap_total(1).wait_recv()
    finish(1, 0, 256)
    swap_total(2).wait_recv()
    finish(1, 256, 128)
    for copy in started:
        copy.wait_send()
    rest = landed_ref.at[pl.ds(0, DEVICES - 1)]
    pltpu.make_async_copy(rest, rest, all_send.at[1]).wait()
    save_rho.wait()
    save_xc.wait()
    for save in saves:
        save.wait()


def whole(shift, scale, flag, count, weights, tiles, density, basis, core_matrix):
    dma = pltpu.SemaphoreType.DMA
    tall, wide = core_matrix.shape
    points, width = basis.shape
    vmem = pl.BlockSpec(memory_space=pltpu.VMEM)
    smem = pl.BlockSpec(memory_space=pltpu.SMEM)
    hbm = pl.BlockSpec(memory_space=pl.ANY)
    bf16, f32 = jnp.bfloat16, jnp.float32
    return pl.pallas_call(
        whole_kernel,
        name="whole_kernel",
        out_shape=(
            jax.ShapeDtypeStruct((1, points), f32),
            jax.ShapeDtypeStruct((tall, wide), f32),
            jax.ShapeDtypeStruct((BS, TILE, wide), f32),
        ),
        in_specs=[smem, smem, smem, smem, vmem, hbm, hbm, hbm, hbm],
        out_specs=(hbm, hbm, hbm),
        scratch_shapes=[
            pltpu.SMEM((BLK, DEVICES), jnp.int32),
            pltpu.VMEM((BLK, DEVICES), jnp.int32),
            pltpu.VMEM((BLK, DEVICES), jnp.int32),
            pltpu.SMEM((BLK, DEVICES), jnp.int32),
            pltpu.VMEM((1, points), f32),
            pltpu.VMEM((tall, wide), f32),
            pltpu.VMEM((BS, TILE, wide), f32),
            pltpu.VMEM((points, width), bf16),
            pltpu.VMEM((BS, TILE, wide), f32),
            pltpu.VMEM((width, points), bf16),
            pltpu.VMEM((width, points), bf16),
            pltpu.VMEM((BS * BS, PART, TILE), bf16),
            pltpu.VMEM((DEVICES, PART, TILE), bf16),
            pltpu.VMEM((2, width // 2, width), bf16),
            pltpu.VMEM((width, width), bf16),
            pltpu.VMEM((DEVICES, PART, TILE), bf16),
            pltpu.VMEM((DEVICES + 1, PART, TILE), f32),
            pltpu.VMEM((BS, PART, 2 * wide), f32),
            pltpu.VMEM((BS * PART, 2 * wide), bf16),
            pltpu.VMEM((2, BS * PART, wide), bf16),
            pltpu.VMEM((BS, PART, wide), jnp.int16),
            pltpu.VMEM((BS, PART, wide), jnp.int16),
            pltpu.VMEM((8, TILE), f32),
            pltpu.VMEM((8, TILE), f32),
            pltpu.VMEM((BS, PART, wide), bf16),
            pltpu.VMEM((BS, PART, wide), bf16),
            pltpu.VMEM((2, RING, PART, wide), bf16),
            pltpu.VMEM((RING, RING, PART, wide), bf16),
            pltpu.VMEM((RING, RING, BS * PART, wide), bf16),
            pltpu.VMEM((RING, 2, BS * PART, 2 * wide), bf16),
            pltpu.VMEM((2, BS * PART, 2 * wide), f32),
            pltpu.VMEM((2, BS * PART, wide), bf16),
            pltpu.VMEM((2, BS * PART, wide), bf16),
            dma((6,)),
            dma((BS // 2,)),
            dma((BS // 2,)),
            dma((BS // 2,)),
            dma((3,)),
            dma((3,)),
            dma((3,)),
            dma((3,)),
            dma((2,)),
            dma((2,)),
            dma((2,)),
            dma((len(JOBS), RING, 2)),
            dma((len(JOBS), RING, 2)),
            dma((RING,)),
            dma((RING,)),
            dma((RING, 2)),
            dma((RING, 2)),
            dma((RING,)),
            dma((RING,)),
            dma((4,)),
            dma((RING, 2)),
            dma((RING, 2)),
            dma((RING,)),
            dma((RING,)),
            dma,
        ],
        compiler_params=pltpu.CompilerParams(
            collective_id=1, has_side_effects=True, vmem_limit_bytes=56 * 2**20
        ),
        cost_estimate=pl.CostEstimate(
            flops=4 * points * width * width + 2 * tall * wide * tall * 8, bytes_accessed=16 * 2**20, transcendentals=0
        ),
    )(shift, scale, flag, count, weights, tiles, density.reshape(BS, TILE, wide), basis, core_matrix.reshape(BS, TILE, wide))


def keep_kernel(*refs):
    count = (len(refs) - 1) // 3
    sems = refs[-1]
    loads, saves = [], []
    for i in range(count):
        source, target, held = refs[i], refs[count + i], refs[2 * count + i]
        parts = 4 if source.shape[0] > 1 else 1
        size = source.shape[0] // parts
        for part in range(parts):
            spot = pl.ds(part * size, size)
            loads.append(pltpu.make_async_copy(source.at[spot], held.at[spot], sems.at[0, i, part]))
            saves.append(pltpu.make_async_copy(held.at[spot], target.at[spot], sems.at[1, i, part]))
    for load in loads:
        load.start()
    for load, save in zip(loads, saves):
        load.wait()
        save.start()
    for save in saves:
        save.wait()


def kept(*arrays):
    hbm = pl.BlockSpec(memory_space=pl.ANY)
    return pl.pallas_call(
        keep_kernel,
        name="keep_kernel",
        out_shape=tuple(jax.ShapeDtypeStruct(a.shape, a.dtype) for a in arrays),
        in_specs=[hbm] * len(arrays),
        out_specs=(hbm,) * len(arrays),
        scratch_shapes=[pltpu.VMEM(a.shape, a.dtype) for a in arrays] + [pltpu.SemaphoreType.DMA((2, len(arrays), 4))],
    )(*arrays)


def body(
    basis_values,
    quad_weights,
    point_counts,
    basis_tiles,
    density,
    core_matrix,
    map_shift,
    map_scale,
    branch_flags,
):
    density_out, potential, purified = whole(
        map_shift,
        map_scale,
        branch_flags,
        point_counts,
        quad_weights,
        basis_tiles.T,
        density,
        basis_values[0],
        core_matrix,
    )
    return kept(density_out, potential, purified.reshape(core_matrix.shape))


def solution(mesh):
    placed = (
        P(("row", "col"), None, None),
        P(("row", "col"), None),
        P(("row", "col")),
        P(),
        P("row", "col"),
        P("row", "col"),
        P(),
        P(),
        P(),
    )
    return jax.shard_map(
        body,
        mesh=mesh,
        in_specs=placed,
        out_specs=(P(("row", "col"), None), P("row", "col"), P("row", "col")),
        check_vma=False,
    )
```
